256 devices in a mesh: lat: 8 (over y, x_hi), lon: 32 (over x_lo, z, core).
Axes of the slice: x: 4 (x_hi: 2, x_lo: 2; x = x_hi * 2 + x_lo), y: 4, z: 8, core: 2. Of those that a mesh axis runs over, the one named last changes fastest.
Arguments:
- latent: bfloat16 [2, 96, 192, 512], P(None, 'lat', 'lon'), may hold values from -40 to 40
- cotangent: bfloat16 [2, 96, 192, 512], P(None, 'lat', 'lon'), may hold values from -6 to 6
- norm_gain: float32 [512], replicated, may hold values from 0.25 to 1.75
- qkv_weight: bfloat16 [512, 1536], replicated, may hold values from -1 to 1
- out_weight: bfloat16 [512, 512], replicated, may hold values from -0.25 to 0.25
Outputs:
- updated: bfloat16 [2, 96, 192, 512], P(None, 'lat', 'lon')
- latent_grad: bfloat16 [2, 96, 192, 512], P(None, 'lat', 'lon')
The draws below stay inside these ranges and needn't reach their ends.
All inputs are finite; a program needn't handle non-finite values.
Results may differ from the reference program's by a relative error of at most 0.022.
Values may be sent and summed in bfloat16 or wider, within the bound.
No kernel may reach another device: no remote copies, remote signals or barrier semaphores. Data moves between devices by JAX's collectives and lax.ppermute only.
A program may use at most 64 MiB of HBM per device.

```python
import math
import jax
import jax.numpy as jnp
from jax import lax

D = 512
HEADS = 8
LEV = 2
WLAT = 12
WLON = 6
SLAT = 6
SLON = 3
NLAT = 96
NLON = 192


def draw_latent(key, part):
    key = jax.random.fold_in(key, 11)
    noise_key = jax.random.fold_in(key, 0)
    noise_field = jnp.clip(jax.random.normal(noise_key, (LEV, NLAT, NLON, D), jnp.float32), -4.0, 4.0)
    return noise_field.astype(jnp.bfloat16)


def draw_qkv_weight(key, part):
    key = jax.random.fold_in(key, 23)
    first_key, second_key, third_key = jax.random.split(key, 3)
    weight_scale = D ** (-0.5)
    query_part = jnp.clip(jax.random.normal(first_key, (D, D), jnp.float32), -4.0, 4.0)
    key_part = jnp.clip(jax.random.normal(second_key, (D, D), jnp.float32), -4.0, 4.0)
    value_part = jnp.clip(jax.random.normal(third_key, (D, D), jnp.float32), -4.0, 4.0)
    return (jnp.concatenate([query_part, key_part, value_part], axis=1) * weight_scale).astype(jnp.bfloat16)


def block_levels(stream_key, extent, cuts, low, top_value):
    def one(axis_at, parts):
        draws = jax.random.uniform(jax.random.fold_in(jax.random.fold_in(stream_key, 6), axis_at), (parts,), jnp.float32, low / len(cuts), top_value / len(cuts))
        return jnp.repeat(jnp.exp(draws), extent[axis_at] // parts).reshape((-1,) + (1,) * (len(extent) - axis_at - 1))

    gain = one(*cuts[0])
    for cut in cuts[1:]:
        gain = gain * one(*cut)
    return gain


def gaussian(stream_key, extent, spread, reach, shards=(), kind=jnp.bfloat16):
    result = spread * jax.random.normal(stream_key, extent, jnp.float32)
    if shards:
        result = result * block_levels(stream_key, extent, shards, -0.22, 0.18)
    return jnp.clip(result, -reach, reach).astype(kind)


def setup_inputs(seed: int = 0) -> dict:
    seeds = jax.random.split(jax.random.key(seed), 6)
    latent = draw_latent(jax.random.fold_in(seeds[5], 71), 0)
    cotangent = gaussian(seeds[1], (LEV, NLAT, NLON, D), 1.0, 6.0, ((1, 8), (2, 32)))
    norm_gain = jnp.clip(1.0 + 0.15 * jax.random.normal(seeds[2], (D,), jnp.float32), 0.25, 1.75)
    qkv_weight = draw_qkv_weight(jax.random.fold_in(seeds[5], 71), 0)
    out_weight = gaussian(seeds[4], (D, D), D ** -0.5, 0.25)
    return {"latent": latent, "cotangent": cotangent, "norm_gain": norm_gain, "qkv_weight": qkv_weight, "out_weight": out_weight}


NORM_EPS = 1e-05
MASK_FILL = -1000000000.0

def to_windows(field):
    levels, lat_rows, lon_cols, features = field.shape
    field = field.reshape(levels, lat_rows // WLAT, WLAT, lon_cols // WLON, WLON, features)
    field = field.transpose(1, 3, 0, 2, 4, 5)
    return field.reshape(lat_rows // WLAT, lon_cols // WLON, levels * WLAT * WLON, features)

def from_windows(blocks, levels):
    row_blocks, col_blocks, window, features = blocks.shape
    blocks = blocks.reshape(row_blocks, col_blocks, levels, WLAT, WLON, features)
    blocks = blocks.transpose(2, 0, 3, 1, 4, 5)
    return blocks.reshape(levels, row_blocks * WLAT, col_blocks * WLON, features)

def region_tokens(global_rows, total_rows, levels, col_blocks):
    region_rows = (global_rows >= total_rows - WLAT).astype(jnp.int32) + (global_rows >= total_rows - SLAT).astype(jnp.int32)
    row_blocks = region_rows.shape[0] // WLAT
    region = jnp.broadcast_to(region_rows.reshape(row_blocks, 1, 1, WLAT, 1), (row_blocks, col_blocks, levels, WLAT, WLON))
    return region.reshape(row_blocks, col_blocks, levels * WLAT * WLON)

def attend(tokens, region, qkv_weight, out_weight, heads):
    count, window, features = tokens.shape
    head_dim = features // heads
    projected = jnp.dot(tokens.reshape(count * window, features), qkv_weight, preferred_element_type=jnp.float32)
    projected = projected.astype(jnp.bfloat16).reshape(count, window, 3, heads, head_dim)
    query_heads = projected[:, :, 0]
    key_heads = projected[:, :, 1]
    value_heads = projected[:, :, 2]
    bias = jnp.where(region[:, :, None] != region[:, None, :], MASK_FILL, 0.0).astype(jnp.float32)
    scores = jnp.einsum('bqhd,bkhd->bhqk', query_heads.astype(jnp.float32), key_heads.astype(jnp.float32))
    scores = scores / math.sqrt(head_dim) + bias[:, None]
    probs = jax.nn.softmax(scores, axis=-1)
    probs_low = probs.astype(jnp.bfloat16)
    mixed = jnp.einsum('bhqk,bkhd->bqhd', probs_low.astype(jnp.float32), value_heads.astype(jnp.float32)).astype(jnp.bfloat16)
    output = jnp.dot(mixed.reshape(count * window, features), out_weight, preferred_element_type=jnp.float32).astype(jnp.bfloat16)
    return ((query_heads, key_heads, value_heads, probs, probs_low), output.reshape(count, window, features))

def attend_back(saved, grad_out, qkv_weight, out_weight):
    query_heads, key_heads, value_heads, probs, probs_low = saved
    count, window, heads, head_dim = query_heads.shape
    features = heads * head_dim
    grad_mixed = jnp.dot(grad_out.reshape(count * window, features), out_weight.T, preferred_element_type=jnp.float32)
    grad_mixed = grad_mixed.astype(jnp.bfloat16).reshape(count, window, heads, head_dim).astype(jnp.float32)
    grad_probs = jnp.einsum('bqhd,bkhd->bhqk', grad_mixed, value_heads.astype(jnp.float32))
    grad_value = jnp.einsum('bhqk,bqhd->bkhd', probs_low.astype(jnp.float32), grad_mixed)
    grad_scores = probs * (grad_probs - lax.optimization_barrier(jnp.sum(grad_probs * probs, axis=-1, keepdims=True))) / math.sqrt(head_dim)
    grad_scores = grad_scores.astype(jnp.bfloat16).astype(jnp.float32)
    grad_query = jnp.einsum('bhqk,bkhd->bqhd', grad_scores, key_heads.astype(jnp.float32))
    grad_key = jnp.einsum('bhqk,bqhd->bkhd', grad_scores, query_heads.astype(jnp.float32))
    grad_proj = jnp.stack([grad_query, grad_key, grad_value], axis=2).astype(jnp.bfloat16).reshape(count * window, 3 * features)
    grad_tokens = jnp.dot(grad_proj, qkv_weight.T, preferred_element_type=jnp.float32).astype(jnp.bfloat16)
    return grad_tokens.reshape(count, window, features)

def normalize(branch):
    values = branch.astype(jnp.float32)
    centred = values - lax.optimization_barrier(jnp.mean(values, axis=-1, keepdims=True))
    inverse = lax.rsqrt(lax.optimization_barrier(jnp.mean(centred * centred, axis=-1, keepdims=True)) + NORM_EPS)
    return (centred * inverse, inverse)

def post_norm(latent, branch, norm_gain):
    normed, inverse = normalize(branch)
    return (latent.astype(jnp.float32) + norm_gain * normed).astype(jnp.bfloat16)

def norm_grad(branch, cotangent, norm_gain):
    normed, inverse = normalize(branch)
    upstream = norm_gain * cotangent.astype(jnp.float32)
    centre_up = lax.optimization_barrier(jnp.mean(upstream, axis=-1, keepdims=True))
    along = lax.optimization_barrier(jnp.mean(upstream * normed, axis=-1, keepdims=True))
    return (inverse * (upstream - centre_up - normed * along)).astype(jnp.bfloat16)

def reference(latent, cotangent, norm_gain, qkv_weight, out_weight):
    levels, total_rows, total_cols, features = latent.shape
    global_rows = jnp.arange(total_rows, dtype=jnp.int32)
    region = region_tokens(global_rows, total_rows, levels, total_cols // WLON)
    shifted = jnp.roll(latent, (-SLAT, -SLON), axis=(1, 2))
    blocks = to_windows(shifted)

    def forward_row(item):
        row_tokens, row_region = item
        return attend(row_tokens, row_region, qkv_weight, out_weight, HEADS)[1]
    branch_blocks = lax.map(forward_row, (blocks, region))
    branch = jnp.roll(from_windows(branch_blocks, levels), (SLAT, SLON), axis=(1, 2))
    updated = post_norm(latent, branch, norm_gain)
    grad_branch = norm_grad(branch, cotangent, norm_gain)
    grad_in = to_windows(jnp.roll(grad_branch, (-SLAT, -SLON), axis=(1, 2)))

    def backward_row(item):
        row_tokens, row_grad, row_region = item
        saved = attend(row_tokens, row_region, qkv_weight, out_weight, HEADS)[0]
        return attend_back(saved, row_grad, qkv_weight, out_weight)
    grad_blocks = lax.map(backward_row, (blocks, grad_in, region))
    grad_attn = jnp.roll(from_windows(grad_blocks, levels), (SLAT, SLON), axis=(1, 2))
    latent_grad = (cotangent.astype(jnp.float32) + grad_attn.astype(jnp.float32)).astype(jnp.bfloat16)
    return (updated, latent_grad)
```

```python
import math

import jax
import jax.numpy as jnp
from jax import lax
from jax.experimental import pallas as pl
from jax.experimental.pallas import tpu as pltpu
from jax.sharding import PartitionSpec as P

HEADS = 8
WLAT = 12
WLON = 6
SLAT = 6
SLON = 3

NORM_EPS = 1e-05
MASK_FILL = -1000000000.0


def neighbour(piece, lat_by, lon_by):
    lats, lons = lax.axis_size("lat"), lax.axis_size("lon")
    pairs = [
        (i * lons + j, (i + lat_by) % lats * lons + (j + lon_by) % lons)
        for i in range(lats)
        for j in range(lons)
    ]
    return lax.ppermute(piece, ("lat", "lon"), pairs)


def row_slices(rows, cols):
    late_rows, late_cols = pl.ds(SLAT, rows - SLAT), pl.ds(SLON, cols - SLON)
    early_rows, early_cols = pl.ds(0, SLAT), pl.ds(0, SLON)
    return (
        (late_rows, late_cols),
        (late_rows, early_cols),
        (early_rows, late_cols),
        (early_rows, early_cols),
    )


def cut_kernel(latent, cotangent, *rest):
    quarters, sems = rest[:4], rest[4]
    copies = []
    for k, (rows, cols) in enumerate(row_slices(latent.shape[0], latent.shape[1])):
        for f, field in enumerate((latent, cotangent)):
            copies.append(
                pltpu.make_async_copy(field.at[rows, cols], quarters[k].at[f], sems.at[k, f])
            )
    for copy in copies:
        copy.start()
    for copy in copies:
        copy.wait()


def join_kernel(*refs):
    quarters, outs, sems = refs[:4], refs[4:6], refs[6]
    copies = []
    for k, (rows, cols) in enumerate(row_slices(outs[0].shape[0], outs[0].shape[1])):
        for f, field in enumerate(outs):
            copies.append(
                pltpu.make_async_copy(quarters[k].at[f], field.at[rows, cols], sems.at[k, f])
            )
    for copy in copies:
        copy.start()
    for copy in copies:
        copy.wait()


def across(a, b):
    return lax.dot_general(a, b, (((1,), (1,)), ((), ())), preferred_element_type=jnp.float32)


def down(a, b):
    return lax.dot_general(a, b, (((0,), (0,)), ((), ())), preferred_element_type=jnp.float32)


def matmul(a, b):
    return jnp.dot(a, b, preferred_element_type=jnp.float32)


def window_kernel(
    own, ahead_lon, ahead_lat, ahead_both, gain_ref, qkv_ref, out_ref,
    own_out, lon_out, lat_out, both_out,
    tokens, cots, probs_ref, low_ref, proj_ref, mixed_ref, grad_ref,
):
    quarters = (own, ahead_lon, ahead_lat, ahead_both)
    results = (own_out, lon_out, lat_out, both_out)
    _, rows, cols, levels, features = own.shape
    quarter = rows * cols * levels
    window = 4 * quarter
    head_dim = features // HEADS
    scale = 1.0 / math.sqrt(head_dim)

    for k, ref in enumerate(quarters):
        for f, into in enumerate((tokens, cots)):
            for r in range(rows):
                for c in range(cols):
                    at = k * quarter + (r * cols + c) * levels
                    into[at : at + levels, :] = ref[f, r, c].astype(jnp.float32)

    proj_ref[...] = matmul(tokens[...].astype(jnp.bfloat16), qkv_ref[...]).astype(jnp.bfloat16)

    last = lax.axis_index("lat") == lax.axis_size("lat") - 1
    first_half = lambda d: lax.broadcasted_iota(jnp.int32, (window, window), d) < 2 * quarter
    fill = jnp.where(last, MASK_FILL, 0.0).astype(jnp.float32)
    bias = jnp.where(first_half(0) != first_half(1), fill, 0.0)
    lane = lax.broadcasted_iota(jnp.int32, (window, 2 * head_dim), 1)

    def masked(x, e):
        return jnp.where((lane >= head_dim) == bool(e), x, jnp.zeros_like(x))

    for pair in range(HEADS // 2):
        at = 2 * head_dim * pair
        wide = slice(at, at + 2 * head_dim)
        query = proj_ref[:, wide]
        key = proj_ref[:, features + at : features + at + 2 * head_dim]
        value = proj_ref[:, 2 * features + at : 2 * features + at + 2 * head_dim]
        mixed = None
        for e in range(2):
            scores = across(query, masked(key, e)) * scale + bias
            top = jnp.max(scores, axis=-1, keepdims=True)
            grown = jnp.exp(scores - top)
            probs = grown / jnp.sum(grown, axis=-1, keepdims=True)
            low = probs.astype(jnp.bfloat16)
            probs_ref[2 * pair + e] = probs
            low_ref[2 * pair + e] = low
            part = matmul(low, masked(value, e))
            mixed = part if mixed is None else mixed + part
        mixed_ref[:, wide] = mixed.astype(jnp.bfloat16)

    branch = matmul(mixed_ref[...], out_ref[...]).astype(jnp.bfloat16).astype(jnp.float32)
    gain = gain_ref[...]
    centred = branch - jnp.mean(branch, axis=-1, keepdims=True)
    inverse = lax.rsqrt(jnp.mean(centred * centred, axis=-1, keepdims=True) + NORM_EPS)
    normed = centred * inverse
    tokens[...] = tokens[...] + gain * normed
    upstream = gain * cots[...]
    centre_up = jnp.mean(upstream, axis=-1, keepdims=True)
    along = jnp.mean(upstream * normed, axis=-1, keepdims=True)
    grad_branch = (inverse * (upstream - centre_up - normed * along)).astype(jnp.bfloat16)
    mixed_ref[...] = across(grad_branch, out_ref[...]).astype(jnp.bfloat16)

    for pair in range(HEADS // 2):
        at = 2 * head_dim * pair
        wide = slice(at, at + 2 * head_dim)
        query = proj_ref[:, wide]
        key = proj_ref[:, features + at : features + at + 2 * head_dim]
        value = proj_ref[:, 2 * features + at : 2 * features + at + 2 * head_dim]
        grad_mixed = mixed_ref[:, wide]
        sums = [None, None, None]
        for e in range(2):
            probs = probs_ref[2 * pair + e]
            grad_probs = across(grad_mixed, masked(value, e))
            along = jnp.sum(grad_probs * probs, axis=-1, keepdims=True)
            grad_scores = (probs * (grad_probs - along) * scale).astype(jnp.bfloat16)
            parts = (
                matmul(grad_scores, masked(key, e)),
                down(grad_scores, masked(query, e)),
                down(low_ref[2 * pair + e], masked(grad_mixed, e)),
            )
            sums = [p if s is None else s + p for s, p in zip(sums, parts)]
        for part, total in enumerate(sums):
            grad_ref[:, part * features + at : part * features + at + 2 * head_dim] = total.astype(
                jnp.bfloat16
            )

    grad_tokens = across(grad_ref[...], qkv_ref[...]).astype(jnp.bfloat16).astype(jnp.float32)
    cots[...] = cots[...] + grad_tokens

    for k, ref in enumerate(results):
        for f, source in enumerate((tokens, cots)):
            for r in range(rows):
                for c in range(cols):
                    at = k * quarter + (r * cols + c) * levels
                    ref[f, r, c] = source[at : at + levels, :].astype(jnp.bfloat16)


def body(latent, cotangent, norm_gain, qkv_weight, out_weight):
    levels, rows, cols, features = latent.shape
    assert (rows, cols) == (WLAT, WLON) and (2 * SLAT, 2 * SLON) == (WLAT, WLON)
    window = levels * rows * cols
    quarter = (2, SLAT, SLON, levels, features)
    in_vmem = pl.BlockSpec(memory_space=pltpu.VMEM)
    anywhere = pl.BlockSpec(memory_space=pl.ANY)
    copies = pltpu.SemaphoreType.DMA((4, 2))

    own, to_lon, to_lat, to_both = pl.pallas_call(
        cut_kernel,
        in_specs=[anywhere] * 2,
        out_specs=[in_vmem] * 4,
        out_shape=[jax.ShapeDtypeStruct(quarter, jnp.bfloat16)] * 4,
        scratch_shapes=[copies],
        name="cut",
    )(latent.transpose(1, 2, 0, 3), cotangent.transpose(1, 2, 0, 3))

    from_both = neighbour(to_both, -1, -1)
    from_lat = neighbour(to_lat, -1, 0)
    from_lon = neighbour(to_lon, 0, -1)

    own, to_lon, to_lat, to_both = pl.pallas_call(
        window_kernel,
        in_specs=[in_vmem] * 7,
        out_specs=[in_vmem] * 4,
        out_shape=[jax.ShapeDtypeStruct(quarter, jnp.bfloat16)] * 4,
        scratch_shapes=[
            pltpu.VMEM((window, features), jnp.float32),
            pltpu.VMEM((window, features), jnp.float32),
            pltpu.VMEM((HEADS, window, window), jnp.float32),
            pltpu.VMEM((HEADS, window, window), jnp.bfloat16),
            pltpu.VMEM((window, 3 * features), jnp.bfloat16),
            pltpu.VMEM((window, features), jnp.bfloat16),
            pltpu.VMEM((window, 3 * features), jnp.bfloat16),
        ],
        compiler_params=pltpu.CompilerParams(vmem_limit_bytes=32 * 1024 * 1024),
        name="window",
    )(own, from_lon, from_lat, from_both, norm_gain.reshape(1, features), qkv_weight, out_weight)

    from_both = neighbour(to_both, 1, 1)
    from_lat = neighbour(to_lat, 1, 0)
    from_lon = neighbour(to_lon, 0, 1)

    updated, latent_grad = pl.pallas_call(
        join_kernel,
        in_specs=[in_vmem] * 4,
        out_specs=[anywhere] * 2,
        out_shape=[jax.ShapeDtypeStruct((rows, cols, levels, features), jnp.bfloat16)] * 2,
        scratch_shapes=[copies],
        name="join",
    )(own, from_lon, from_lat, from_both)
    return (updated.transpose(2, 0, 1, 3), latent_grad.transpose(2, 0, 1, 3))


def solution(mesh):
    placed = (P(None, "lat", "lon", None), P(None, "lat", "lon", None), P(), P(), P())
    return jax.shard_map(
        body,
        mesh=mesh,
        in_specs=placed,
        out_specs=(P(None, "lat", "lon", None), P(None, "lat", "lon", None)),
        check_vma=False,
    )
```

```python
import math

import jax
import jax.numpy as jnp
from jax import lax
from jax.experimental import pallas as pl
from jax.experimental.pallas import tpu as pltpu
from jax.sharding import PartitionSpec as P

HEADS = 8
WLAT = 12
WLON = 6
SLAT = 6
SLON = 3

MIB = 1 << 20
NORM_EPS = 1e-05
MASK_FILL = -1000000000.0


def neighbour(piece, lat_by, lon_by):
    lats, lons = lax.axis_size("lat"), lax.axis_size("lon")
    pairs = [
        (i * lons + j, (i + lat_by) % lats * lons + (j + lon_by) % lons)
        for i in range(lats)
        for j in range(lons)
    ]
    return lax.ppermute(piece, ("lat", "lon"), pairs)


def row_slices(rows, cols):
    late_rows, late_cols = pl.ds(SLAT, rows - SLAT), pl.ds(SLON, cols - SLON)
    early_rows, early_cols = pl.ds(0, SLAT), pl.ds(0, SLON)
    return (
        (late_rows, late_cols),
        (late_rows, early_cols),
        (early_rows, late_cols),
        (early_rows, early_cols),
    )


def stay(x):
    return pltpu.with_memory_space_constraint(x, pltpu.HBM)


def cut_kernel(latent, cotangent, *rest):
    pieces, sems = rest[:3], rest[3]
    copies = []
    for k, (rows, cols) in enumerate(row_slices(latent.shape[0], latent.shape[1])[1:]):
        for f, field in enumerate((latent, cotangent)):
            copies.append(
                pltpu.make_async_copy(field.at[rows, cols], pieces[k].at[f], sems.at[k, f])
            )
    for copy in copies:
        copy.start()
    for copy in copies:
        copy.wait()


def fetch_kernel(latent, cotangent, gain, qkv, out, own, gain_to, qkv_to, out_to, sems):
    rows, cols = row_slices(latent.shape[0], latent.shape[1])[0]
    copies = [
        pltpu.make_async_copy(qkv, qkv_to, sems.at[0]),
        pltpu.make_async_copy(out, out_to, sems.at[1]),
        pltpu.make_async_copy(gain, gain_to, sems.at[2]),
        pltpu.make_async_copy(latent.at[rows, cols], own.at[0], sems.at[3]),
        pltpu.make_async_copy(cotangent.at[rows, cols], own.at[1], sems.at[4]),
    ]
    for copy in copies:
        copy.start()
    for copy in copies:
        copy.wait()


def join_kernel(*refs):
    quarters, outs, sems = refs[3::-1], refs[4:6], refs[6]
    copies = []
    for k, (rows, cols) in enumerate(row_slices(outs[0].shape[0], outs[0].shape[1])):
        for f, field in enumerate(outs):
            copies.append(
                pltpu.make_async_copy(quarters[k].at[f], field.at[rows, cols], sems.at[k, f])
            )
    for copy in copies:
        copy.start()
    for copy in copies:
        copy.wait()


def across(a, b):
    return lax.dot_general(a, b, (((1,), (1,)), ((), ())), preferred_element_type=jnp.float32)


def down(a, b):
    return lax.dot_general(a, b, (((0,), (0,)), ((), ())), preferred_element_type=jnp.float32)


def matmul(a, b):
    return jnp.dot(a, b, preferred_element_type=jnp.float32)


def window_kernel(
    ahead_both, ahead_lat, ahead_lon, own, gain_ref, qkv_ref, out_ref,
    both_out, lat_out, lon_out, own_out,
    tokens, cots, probs_ref, low_ref, proj_ref, mixed_ref, grad_ref,
):
    quarters = (own, ahead_lon, ahead_lat, ahead_both)
    results = (own_out, lon_out, lat_out, both_out)
    _, rows, cols, levels, features = own.shape
    quarter = rows * cols * levels
    window = 4 * quarter
    head_dim = features // HEADS
    scale = 1.0 / math.sqrt(head_dim)

    for k, ref in enumerate(quarters):
        for f, into in enumerate((tokens, cots)):
            for r in range(rows):
                for c in range(cols):
                    at = k * quarter + (r * cols + c) * levels
                    into[at : at + levels, :] = ref[f, r, c].astype(jnp.float32)

    proj_ref[...] = matmul(tokens[...].astype(jnp.bfloat16), qkv_ref[...]).astype(jnp.bfloat16)

    last = lax.axis_index("lat") == lax.axis_size("lat") - 1
    first_half = lambda d: lax.broadcasted_iota(jnp.int32, (window, window), d) < 2 * quarter
    fill = jnp.where(last, MASK_FILL, 0.0).astype(jnp.float32)
    bias = jnp.where(first_half(0) != first_half(1), fill, 0.0)
    lane = lax.broadcasted_iota(jnp.int32, (window, 2 * head_dim), 1)

    def masked(x, e):
        return jnp.where((lane >= head_dim) == bool(e), x, jnp.zeros_like(x))

    for pair in range(HEADS // 2):
        at = 2 * head_dim * pair
        wide = slice(at, at + 2 * head_dim)
        query = proj_ref[:, wide]
        key = proj_ref[:, features + at : features + at + 2 * head_dim]
        value = proj_ref[:, 2 * features + at : 2 * features + at + 2 * head_dim]
        mixed = None
        for e in range(2):
            scores = across(query, masked(key, e)) * scale + bias
            top = jnp.max(scores, axis=-1, keepdims=True)
            grown = jnp.exp(scores - top)
            probs = grown / jnp.sum(grown, axis=-1, keepdims=True)
            low = probs.astype(jnp.bfloat16)
            probs_ref[2 * pair + e] = probs
            low_ref[2 * pair + e] = low
            part = matmul(low, masked(value, e))
            mixed = part if mixed is None else mixed + part
        mixed_ref[:, wide] = mixed.astype(jnp.bfloat16)

    branch = matmul(mixed_ref[...], out_ref[...]).astype(jnp.bfloat16).astype(jnp.float32)
    gain = gain_ref[...]
    centred = branch - jnp.mean(branch, axis=-1, keepdims=True)
    inverse = lax.rsqrt(jnp.mean(centred * centred, axis=-1, keepdims=True) + NORM_EPS)
    normed = centred * inverse
    tokens[...] = tokens[...] + gain * normed
    upstream = gain * cots[...]
    centre_up = jnp.mean(upstream, axis=-1, keepdims=True)
    along = jnp.mean(upstream * normed, axis=-1, keepdims=True)
    grad_branch = (inverse * (upstream - centre_up - normed * along)).astype(jnp.bfloat16)
    mixed_ref[...] = across(grad_branch, out_ref[...]).astype(jnp.bfloat16)

    for pair in range(HEADS // 2):
        at = 2 * head_dim * pair
        wide = slice(at, at + 2 * head_dim)
        query = proj_ref[:, wide]
        key = proj_ref[:, features + at : features + at + 2 * head_dim]
        value = proj_ref[:, 2 * features + at : 2 * features + at + 2 * head_dim]
        grad_mixed = mixed_ref[:, wide]
        sums = [None, None, None]
        for e in range(2):
            probs = probs_ref[2 * pair + e]
            grad_probs = across(grad_mixed, masked(value, e))
            along = jnp.sum(grad_probs * probs, axis=-1, keepdims=True)
            grad_scores = (probs * (grad_probs - along) * scale).astype(jnp.bfloat16)
            parts = (
                matmul(grad_scores, masked(key, e)),
                down(grad_scores, masked(query, e)),
                down(low_ref[2 * pair + e], masked(grad_mixed, e)),
            )
            sums = [p if s is None else s + p for s, p in zip(sums, parts)]
        for part, total in enumerate(sums):
            grad_ref[:, part * features + at : part * features + at + 2 * head_dim] = total.astype(
                jnp.bfloat16
            )

    grad_tokens = across(grad_ref[...], qkv_ref[...]).astype(jnp.bfloat16).astype(jnp.float32)
    cots[...] = cots[...] + grad_tokens

    for k, ref in enumerate(results):
        for f, source in enumerate((tokens, cots)):
            for r in range(rows):
                for c in range(cols):
                    at = k * quarter + (r * cols + c) * levels
                    ref[f, r, c] = source[at : at + levels, :].astype(jnp.bfloat16)


def body(latent, cotangent, norm_gain, qkv_weight, out_weight):
    levels, rows, cols, features = latent.shape
    assert (rows, cols) == (WLAT, WLON) and (2 * SLAT, 2 * SLON) == (WLAT, WLON)
    window = levels * rows * cols
    quarter = (2, SLAT, SLON, levels, features)
    in_vmem = pl.BlockSpec(memory_space=pltpu.VMEM)
    in_hbm = pl.BlockSpec(memory_space=pltpu.HBM)
    piece = pltpu.VMEM(quarter, jnp.bfloat16)
    few = pltpu.CompilerParams(vmem_limit_bytes=MIB)
    latent, cotangent = latent.transpose(1, 2, 0, 3), cotangent.transpose(1, 2, 0, 3)

    to_lon, to_lat, to_both = pl.pallas_call(
        cut_kernel,
        in_specs=[in_hbm] * 2,
        out_specs=[in_vmem] * 3,
        out_shape=[piece] * 3,
        scratch_shapes=[pltpu.SemaphoreType.DMA((3, 2))],
        compiler_params=few,
        name="cut",
    )(stay(latent), stay(cotangent))

    from_both = neighbour(to_both, -1, -1)
    from_lat = neighbour(to_lat, -1, 0)
    from_lon = neighbour(to_lon, 0, -1)

    own, gain, qkv, out = pl.pallas_call(
        fetch_kernel,
        in_specs=[in_hbm] * 5,
        out_specs=[in_vmem] * 4,
        out_shape=[
            piece,
            pltpu.VMEM((1, features), jnp.float32),
            pltpu.VMEM(qkv_weight.shape, jnp.bfloat16),
            pltpu.VMEM(out_weight.shape, jnp.bfloat16),
        ],
        scratch_shapes=[pltpu.SemaphoreType.DMA((5,))],
        compiler_params=few,
        cost_estimate=pl.CostEstimate(flops=0, bytes_accessed=4 * MIB, transcendentals=0),
        name="fetch",
    )(*map(stay, (latent, cotangent, norm_gain.reshape(1, features), qkv_weight, out_weight)))

    to_both, to_lat, to_lon, own = pl.pallas_call(
        window_kernel,
        in_specs=[in_vmem] * 7,
        out_specs=[in_vmem] * 4,
        out_shape=[piece] * 4,
        scratch_shapes=[
            pltpu.VMEM((window, features), jnp.float32),
            pltpu.VMEM((window, features), jnp.float32),
            pltpu.VMEM((HEADS, window, window), jnp.float32),
            pltpu.VMEM((HEADS, window, window), jnp.bfloat16),
            pltpu.VMEM((window, 3 * features), jnp.bfloat16),
            pltpu.VMEM((window, features), jnp.bfloat16),
            pltpu.VMEM((window, 3 * features), jnp.bfloat16),
        ],
        compiler_params=pltpu.CompilerParams(vmem_limit_bytes=12 * MIB),
        name="window",
    )(from_both, from_lat, from_lon, own, gain, qkv, out)

    from_both = neighbour(to_both, 1, 1)
    from_lat = neighbour(to_lat, 1, 0)
    from_lon = neighbour(to_lon, 0, 1)

    updated, latent_grad = pl.pallas_call(
        join_kernel,
        in_specs=[in_vmem] * 4,
        out_specs=[in_hbm] * 2,
        out_shape=[jax.ShapeDtypeStruct((rows, cols, levels, features), jnp.bfloat16)] * 2,
        scratch_shapes=[pltpu.SemaphoreType.DMA((4, 2))],
        compiler_params=few,
        name="join",
    )(from_both, from_lat, from_lon, own)
    return (updated.transpose(2, 0, 1, 3), latent_grad.transpose(2, 0, 1, 3))


def solution(mesh):
    placed = (P(None, "lat", "lon", None), P(None, "lat", "lon", None), P(), P(), P())
    return jax.shard_map(
        body,
        mesh=mesh,
        in_specs=placed,
        out_specs=(P(None, "lat", "lon", None), P(None, "lat", "lon", None)),
        check_vma=False,
    )
```

```python
import math

import jax
import jax.numpy as jnp
from jax import lax
from jax.experimental import pallas as pl
from jax.experimental.pallas import tpu as pltpu
from jax.sharding import PartitionSpec as P

HEADS = 8
WLAT = 12
WLON = 6
SLAT = 6
SLON = 3

MIB = 1 << 20
NORM_EPS = 1e-05
MASK_FILL = -1000000000.0

LAT_STEP = 1
LON_STEP = 1


def neighbour(piece, lat_by, lon_by):
    lats, lons = lax.axis_size("lat"), lax.axis_size("lon")
    pairs = [
        (i * lons + j, (i + lat_by) % lats * lons + (j + lon_by) % lons)
        for i in range(lats)
        for j in range(lons)
    ]
    return lax.ppermute(piece, ("lat", "lon"), pairs)


def corners(rows, cols):
    early_rows, late_rows = pl.ds(0, SLAT), pl.ds(SLAT, rows - SLAT)
    early_cols, late_cols = pl.ds(0, SLON), pl.ds(SLON, cols - SLON)
    go_rows, stay_rows = (early_rows, late_rows) if LAT_STEP < 0 else (late_rows, early_rows)
    go_cols, stay_cols = (early_cols, late_cols) if LON_STEP < 0 else (late_cols, early_cols)
    return (
        (go_rows, go_cols), (go_rows, stay_cols), (stay_rows, go_cols), (stay_rows, stay_cols)
    )


def stay(x):
    return pltpu.with_memory_space_constraint(x, pltpu.HBM)


def cut_kernel(latent, cotangent, *rest):
    pieces, sems = rest[:3], rest[3]
    copies = []
    for k, (rows, cols) in enumerate(corners(*latent.shape[:2])[:3]):
        for f, field in enumerate((latent, cotangent)):
            copies.append(
                pltpu.make_async_copy(field.at[rows, cols], pieces[k].at[f], sems.at[k, f])
            )
    for copy in copies:
        copy.start()
    for copy in copies:
        copy.wait()


def fetch_kernel(
    latent, cotangent, gain, qkv, out, own, gain_to, qkv_to, out_to, qkv_turned, out_turned, sems
):
    rows, cols = corners(*latent.shape[:2])[3]
    copies = [
        pltpu.make_async_copy(qkv, qkv_to, sems.at[0]),
        pltpu.make_async_copy(out, out_to, sems.at[1]),
        pltpu.make_async_copy(gain, gain_to, sems.at[2]),
        pltpu.make_async_copy(latent.at[rows, cols], own.at[0], sems.at[3]),
        pltpu.make_async_copy(cotangent.at[rows, cols], own.at[1], sems.at[4]),
    ]
    for copy in copies:
        copy.start()
    copies[1].wait()
    out_turned[...] = out_to[...].T
    copies[0].wait()
    qkv_turned[...] = qkv_to[...].T
    for copy in copies[2:]:
        copy.wait()


def join_kernel(*refs):
    quarters, outs, sems = refs[:4], refs[4:6], refs[6]
    copies = []
    for k, (rows, cols) in enumerate(corners(*outs[0].shape[:2])):
        for f, field in enumerate(outs):
            copies.append(
                pltpu.make_async_copy(quarters[k].at[f], field.at[rows, cols], sems.at[k, f])
            )
    for copy in copies:
        copy.start()
    for copy in copies:
        copy.wait()


def across(a, b):
    return lax.dot_general(a, b, (((1,), (1,)), ((), ())), preferred_element_type=jnp.float32)


def down(a, b):
    return lax.dot_general(a, b, (((0,), (0,)), ((), ())), preferred_element_type=jnp.float32)


def matmul(a, b):
    return jnp.dot(a, b, preferred_element_type=jnp.float32)


def window_kernel(
    ahead_both, ahead_lat, ahead_lon, own, gain_ref, qkv_ref, out_ref, qkv_turned, out_turned,
    both_out, lat_out, lon_out, own_out,
    tokens, cots, scores_ref, low_ref, slopes_ref, proj_ref, mixed_ref, grad_ref,
):
    quarters = (ahead_both, ahead_lat, ahead_lon, own)
    results = (both_out, lat_out, lon_out, own_out)
    _, rows, cols, levels, features = own.shape
    quarter = rows * cols * levels
    window = 4 * quarter
    head_dim = features // HEADS
    wide = 2 * head_dim
    scale = 1.0 / math.sqrt(head_dim)

    for k, ref in enumerate(quarters):
        for f, into in enumerate((tokens, cots)):
            for r in range(rows):
                for c in range(cols):
                    at = k * quarter + (r * cols + c) * levels
                    into[at : at + levels, :] = ref[f, r, c].astype(jnp.float32)

    proj = matmul(tokens[...].astype(jnp.bfloat16), qkv_ref[...]).astype(jnp.bfloat16)
    proj_ref[:, features:] = proj[:, features:]
    proj_ref[:, :features] = proj[:, :features] * jnp.asarray(scale, jnp.bfloat16)

    last = lax.axis_index("lat") == (lax.axis_size("lat") - 1 if LAT_STEP < 0 else 0)
    first_half = lambda d: lax.broadcasted_iota(jnp.int32, (window, window), d) < 2 * quarter
    fill = jnp.where(last, MASK_FILL, 0.0).astype(jnp.float32)
    bias = jnp.where(first_half(0) != first_half(1), fill, 0.0)
    lane = lax.broadcasted_iota(jnp.int32, (1, wide), 1)
    only = [(lane // head_dim == e).astype(jnp.float32).astype(jnp.bfloat16) for e in range(2)]
    second = lax.broadcasted_iota(jnp.int32, (window, wide), 1) >= head_dim

    def part(ref, which, pair):
        at = which * features + wide * pair
        return ref[:, at : at + wide]

    for head in range(HEADS):
        pair, e = divmod(head, 2)
        scores_ref[head] = across(part(proj_ref, 0, pair), part(proj_ref, 1, pair) * only[e])

    for head in range(HEADS):
        scores = scores_ref[head] + bias
        grown = jnp.exp(scores - jnp.max(scores, axis=-1, keepdims=True))
        probs = grown * (1.0 / jnp.sum(grown, axis=-1, keepdims=True))
        scores_ref[head] = probs
        low_ref[head] = probs.astype(jnp.bfloat16)

    for pair in range(HEADS // 2):
        value = part(proj_ref, 2, pair)
        mixed = [matmul(low_ref[2 * pair + e], value) for e in range(2)]
        at = wide * pair
        mixed_ref[:, at : at + wide] = jnp.where(second, mixed[1], mixed[0]).astype(jnp.bfloat16)

    branch = matmul(mixed_ref[...], out_ref[...]).astype(jnp.bfloat16).astype(jnp.float32)
    gain = gain_ref[...]
    centred = branch - jnp.mean(branch, axis=-1, keepdims=True)
    inverse = lax.rsqrt(jnp.mean(centred * centred, axis=-1, keepdims=True) + NORM_EPS)
    normed = centred * inverse
    tokens[...] = tokens[...] + gain * normed
    upstream = gain * cots[...]
    centre_up = jnp.mean(upstream, axis=-1, keepdims=True)
    along = jnp.mean(upstream * normed, axis=-1, keepdims=True)
    grad_branch = (inverse * (upstream - centre_up - normed * along)).astype(jnp.bfloat16)
    mixed_ref[...] = matmul(grad_branch, out_turned[...]).astype(jnp.bfloat16)

    for head in range(HEADS):
        pair, e = divmod(head, 2)
        slopes_ref[head] = across(part(mixed_ref, 0, pair), part(proj_ref, 2, pair) * only[e])

    def put(which, pair, two):
        at = which * features + wide * pair
        grad_ref[:, at : at + wide] = jnp.where(second, two[1], two[0]).astype(jnp.bfloat16)

    for pair in range(HEADS // 2):
        grad_mixed = part(mixed_ref, 0, pair)
        put(2, pair, [down(low_ref[2 * pair + e], grad_mixed) for e in range(2)])

    for head in range(HEADS):
        probs, grad_probs = scores_ref[head], slopes_ref[head]
        along = jnp.sum(grad_probs * probs, axis=-1, keepdims=True)
        low_ref[head] = (probs * (grad_probs - along)).astype(jnp.bfloat16)

    for pair in range(HEADS // 2):
        query, key = part(proj_ref, 0, pair), part(proj_ref, 1, pair)
        put(0, pair, [matmul(low_ref[2 * pair + e], key) * scale for e in range(2)])
        put(1, pair, [down(low_ref[2 * pair + e], query) for e in range(2)])

    grad_tokens = matmul(grad_ref[...], qkv_turned[...]).astype(jnp.bfloat16).astype(jnp.float32)
    cots[...] = cots[...] + grad_tokens

    for k, ref in enumerate(results):
        for f, source in enumerate((tokens, cots)):
            for r in range(rows):
                for c in range(cols):
                    at = k * quarter + (r * cols + c) * levels
                    ref[f, r, c] = source[at : at + levels, :].astype(jnp.bfloat16)


def body(latent, cotangent, norm_gain, qkv_weight, out_weight):
    levels, rows, cols, features = latent.shape
    assert (rows, cols) == (WLAT, WLON) and (2 * SLAT, 2 * SLON) == (WLAT, WLON)
    window = levels * rows * cols
    quarter = (2, SLAT, SLON, levels, features)
    in_vmem = pl.BlockSpec(memory_space=pltpu.VMEM)
    in_hbm = pl.BlockSpec(memory_space=pltpu.HBM)
    piece = pltpu.VMEM(quarter, jnp.bfloat16)
    few = pltpu.CompilerParams(vmem_limit_bytes=MIB)
    latent, cotangent = latent.transpose(1, 2, 0, 3), cotangent.transpose(1, 2, 0, 3)

    to_both, to_lat, to_lon = pl.pallas_call(
        cut_kernel,
        in_specs=[in_hbm] * 2,
        out_specs=[in_vmem] * 3,
        out_shape=[piece] * 3,
        scratch_shapes=[pltpu.SemaphoreType.DMA((3, 2))],
        compiler_params=few,
        name="cut",
    )(stay(latent), stay(cotangent))

    from_both = neighbour(to_both, LAT_STEP, LON_STEP)
    from_lat = neighbour(to_lat, LAT_STEP, 0)
    from_lon = neighbour(to_lon, 0, LON_STEP)

    own, *parameters = pl.pallas_call(
        fetch_kernel,
        in_specs=[in_hbm] * 5,
        out_specs=[in_vmem] * 6,
        out_shape=[
            piece,
            pltpu.VMEM((1, features), jnp.float32),
            pltpu.VMEM(qkv_weight.shape, jnp.bfloat16),
            pltpu.VMEM(out_weight.shape, jnp.bfloat16),
            pltpu.VMEM(qkv_weight.shape[::-1], jnp.bfloat16),
            pltpu.VMEM(out_weight.shape[::-1], jnp.bfloat16),
        ],
        scratch_shapes=[pltpu.SemaphoreType.DMA((5,))],
        compiler_params=few,
        cost_estimate=pl.CostEstimate(flops=0, bytes_accessed=4 * MIB, transcendentals=0),
        name="fetch",
    )(*map(stay, (latent, cotangent, norm_gain.reshape(1, features), qkv_weight, out_weight)))

    to_both, to_lat, to_lon, own = pl.pallas_call(
        window_kernel,
        in_specs=[in_vmem] * 9,
        out_specs=[in_vmem] * 4,
        out_shape=[piece] * 4,
        scratch_shapes=[
            pltpu.VMEM((window, features), jnp.float32),
            pltpu.VMEM((window, features), jnp.float32),
            pltpu.VMEM((HEADS, window, window), jnp.float32),
            pltpu.VMEM((HEADS, window, window), jnp.bfloat16),
            pltpu.VMEM((HEADS, window, window), jnp.float32),
            pltpu.VMEM((window, 3 * features), jnp.bfloat16),
            pltpu.VMEM((window, features), jnp.bfloat16),
            pltpu.VMEM((window, 3 * features), jnp.bfloat16),
        ],
        compiler_params=pltpu.CompilerParams(vmem_limit_bytes=12 * MIB),
        name="window",
    )(from_both, from_lat, from_lon, own, *parameters)

    from_both = neighbour(to_both, -LAT_STEP, -LON_STEP)
    from_lat = neighbour(to_lat, -LAT_STEP, 0)
    from_lon = neighbour(to_lon, 0, -LON_STEP)

    updated, latent_grad = pl.pallas_call(
        join_kernel,
        in_specs=[in_vmem] * 4,
        out_specs=[in_hbm] * 2,
        out_shape=[jax.ShapeDtypeStruct((rows, cols, levels, features), jnp.bfloat16)] * 2,
        scratch_shapes=[pltpu.SemaphoreType.DMA((4, 2))],
        compiler_params=few,
        name="join",
    )(from_both, from_lat, from_lon, own)
    return (updated.transpose(2, 0, 1, 3), latent_grad.transpose(2, 0, 1, 3))


def solution(mesh):
    placed = (P(None, "lat", "lon", None), P(None, "lat", "lon", None), P(), P(), P())
    return jax.shard_map(
        body,
        mesh=mesh,
        in_specs=placed,
        out_specs=(P(None, "lat", "lon", None), P(None, "lat", "lon", None)),
        check_vma=False,
    )
```

```python
import math

import jax
import jax.numpy as jnp
from jax import lax
from jax.experimental import pallas as pl
from jax.experimental.pallas import tpu as pltpu
from jax.sharding import PartitionSpec as P

HEADS = 8
WLAT = 12
WLON = 6
SLAT = 6
SLON = 3
GROUP = 4

MIB = 1 << 20
NORM_EPS = 1e-05
MASK_FILL = -1000000000.0

LAT_STEP = 1
LON_STEP = 1


def neighbour(piece, lat_by, lon_by):
    lats, lons = lax.axis_size("lat"), lax.axis_size("lon")
    pairs = [
        (i * lons + j, (i + lat_by) % lats * lons + (j + lon_by) % lons)
        for i in range(lats)
        for j in range(lons)
    ]
    return lax.ppermute(piece, ("lat", "lon"), pairs)


def corners(rows, cols):
    early_rows, late_rows = pl.ds(0, SLAT), pl.ds(SLAT, rows - SLAT)
    early_cols, late_cols = pl.ds(0, SLON), pl.ds(SLON, cols - SLON)
    go_rows, stay_rows = (early_rows, late_rows) if LAT_STEP < 0 else (late_rows, early_rows)
    go_cols, stay_cols = (early_cols, late_cols) if LON_STEP < 0 else (late_cols, early_cols)
    return (
        (go_rows, go_cols), (go_rows, stay_cols), (stay_rows, go_cols), (stay_rows, stay_cols)
    )


def stay(x):
    return pltpu.with_memory_space_constraint(x, pltpu.HBM)


def cut_kernel(latent, cotangent, *rest):
    pieces, sems = rest[:3], rest[3]
    copies = []
    for k, (rows, cols) in enumerate(corners(*latent.shape[:2])[:3]):
        for f, field in enumerate((latent, cotangent)):
            copies.append(
                pltpu.make_async_copy(field.at[rows, cols], pieces[k].at[f], sems.at[k, f])
            )
    for copy in copies:
        copy.start()
    for copy in copies:
        copy.wait()


def fetch_kernel(
    latent, cotangent, gain, qkv, out, own, gain_to, qkv_to, out_to, qkv_turned, out_turned, sems
):
    rows, cols = corners(*latent.shape[:2])[3]
    copies = [
        pltpu.make_async_copy(qkv, qkv_to, sems.at[0]),
        pltpu.make_async_copy(out, out_to, sems.at[1]),
        pltpu.make_async_copy(gain, gain_to, sems.at[2]),
        pltpu.make_async_copy(latent.at[rows, cols], own.at[0], sems.at[3]),
        pltpu.make_async_copy(cotangent.at[rows, cols], own.at[1], sems.at[4]),
    ]
    for copy in copies:
        copy.start()
    copies[1].wait()
    out_turned[...] = out_to[...].T
    copies[0].wait()
    qkv_turned[...] = qkv_to[...].T
    for copy in copies[2:]:
        copy.wait()


def join_kernel(*refs):
    quarters, outs, sems = refs[:4], refs[4:6], refs[6]
    copies = []
    for k, (rows, cols) in enumerate(corners(*outs[0].shape[:2])):
        for f, field in enumerate(outs):
            copies.append(
                pltpu.make_async_copy(quarters[k].at[f], field.at[rows, cols], sems.at[k, f])
            )
    for copy in copies:
        copy.start()
    for copy in copies:
        copy.wait()


def across(a, b):
    return lax.dot_general(a, b, (((1,), (1,)), ((), ())), preferred_element_type=jnp.float32)


def down(a, b):
    return lax.dot_general(a, b, (((0,), (0,)), ((), ())), preferred_element_type=jnp.float32)


def matmul(a, b):
    return jnp.dot(a, b, preferred_element_type=jnp.float32)


def window_kernel(
    ahead_both, ahead_lat, ahead_lon, own, gain_ref, qkv_ref, out_ref, qkv_turned, out_turned,
    both_out, lat_out, lon_out, own_out,
    tokens, cots, scores_ref, low_ref, slopes_ref, wide_query, proj_ref, mixed_ref, grad_ref,
):
    quarters = (ahead_both, ahead_lat, ahead_lon, own)
    results = (both_out, lat_out, lon_out, own_out)
    _, rows, cols, levels, features = own.shape
    quarter = rows * cols * levels
    window = 4 * quarter
    head_dim = features // HEADS
    scale = 1.0 / math.sqrt(head_dim)

    for k, ref in enumerate(quarters):
        for f, into in enumerate((tokens, cots)):
            for r in range(rows):
                for c in range(cols):
                    at = k * quarter + (r * cols + c) * levels
                    into[at : at + levels, :] = ref[f, r, c].astype(jnp.float32)

    proj = matmul(tokens[...].astype(jnp.bfloat16), qkv_ref[...]).astype(jnp.bfloat16)
    proj_ref[:, features:] = proj[:, features:]
    proj_ref[:, :features] = proj[:, :features] * jnp.asarray(scale, jnp.bfloat16)

    last = lax.axis_index("lat") == (lax.axis_size("lat") - 1 if LAT_STEP < 0 else 0)
    wide = GROUP * head_dim
    packed = GROUP * window
    key_row = lax.broadcasted_iota(jnp.int32, (window, packed), 0)
    query_row = lax.rem(lax.broadcasted_iota(jnp.int32, (window, packed), 1), window)
    fill = jnp.where(last, MASK_FILL, 0.0).astype(jnp.float32)
    bias = jnp.where((key_row < 2 * quarter) != (query_row < 2 * quarter), fill, 0.0)
    lane = lax.broadcasted_iota(jnp.int32, (1, wide), 1)
    only = [(lane // head_dim == e).astype(jnp.float32).astype(jnp.bfloat16) for e in range(GROUP)]
    mine = [lax.broadcasted_iota(jnp.int32, (window, wide), 1) < head_dim * e for e in range(1, GROUP)]

    def part(ref, which, group):
        at = which * features + wide * group
        return ref[:, at : at + wide]

    def fanned(x):
        return jnp.concatenate([x * only[e] for e in range(GROUP)], axis=0)

    def gathered(x):
        out = x[(GROUP - 1) * window :]
        for e in range(GROUP - 2, -1, -1):
            out = jnp.where(mine[e], x[e * window : (e + 1) * window], out)
        return out

    for group in range(HEADS // GROUP):
        wide_query[group] = fanned(part(proj_ref, 0, group))
        scores_ref[group] = across(part(proj_ref, 1, group), wide_query[group])

    for group in range(HEADS // GROUP):
        scores = scores_ref[group] + bias
        grown = jnp.exp(scores - jnp.max(scores, axis=0, keepdims=True))
        probs = grown * (1.0 / jnp.sum(grown, axis=0, keepdims=True))
        scores_ref[group] = probs
        low_ref[group] = probs.astype(jnp.bfloat16)

    for group in range(HEADS // GROUP):
        at = wide * group
        mixed = gathered(down(low_ref[group], part(proj_ref, 2, group)))
        mixed_ref[:, at : at + wide] = mixed.astype(jnp.bfloat16)

    branch = matmul(mixed_ref[...], out_ref[...]).astype(jnp.bfloat16).astype(jnp.float32)
    gain = gain_ref[...]
    upstream = gain * cots[...]
    centre_up = jnp.mean(upstream, axis=-1, keepdims=True)
    centred = branch - jnp.mean(branch, axis=-1, keepdims=True)
    spread = jnp.mean(centred * centred, axis=-1, keepdims=True)
    along = jnp.mean(upstream * centred, axis=-1, keepdims=True)
    inverse = lax.rsqrt(spread + NORM_EPS)
    normed = centred * inverse
    tokens[...] = tokens[...] + gain * normed
    grad_branch = (inverse * (upstream - centre_up - normed * (along * inverse))).astype(jnp.bfloat16)
    mixed_ref[...] = matmul(grad_branch, out_turned[...]).astype(jnp.bfloat16)

    def put(which, group, x):
        at = which * features + wide * group
        grad_ref[:, at : at + wide] = x.astype(jnp.bfloat16)

    for group in range(HEADS // GROUP):
        grad_mixed = fanned(part(mixed_ref, 0, group))
        slopes_ref[group] = across(part(proj_ref, 2, group), grad_mixed)
        put(2, group, matmul(low_ref[group], grad_mixed))

    for group in range(HEADS // GROUP):
        probs, grad_probs = scores_ref[group], slopes_ref[group]
        along = jnp.sum(grad_probs * probs, axis=0, keepdims=True)
        low_ref[group] = (probs * (grad_probs - along)).astype(jnp.bfloat16)

    for group in range(HEADS // GROUP):
        put(0, group, gathered(down(low_ref[group], part(proj_ref, 1, group))) * scale)
        put(1, group, matmul(low_ref[group], wide_query[group]))

    grad_tokens = matmul(grad_ref[...], qkv_turned[...]).astype(jnp.bfloat16).astype(jnp.float32)
    cots[...] = cots[...] + grad_tokens

    for k, ref in enumerate(results):
        for f, source in enumerate((tokens, cots)):
            for r in range(rows):
                for c in range(cols):
                    at = k * quarter + (r * cols + c) * levels
                    ref[f, r, c] = source[at : at + levels, :].astype(jnp.bfloat16)


def body(latent, cotangent, norm_gain, qkv_weight, out_weight):
    levels, rows, cols, features = latent.shape
    assert (rows, cols) == (WLAT, WLON) and (2 * SLAT, 2 * SLON) == (WLAT, WLON)
    window = levels * rows * cols
    quarter = (2, SLAT, SLON, levels, features)
    packed = (HEADS // GROUP, window, GROUP * window)
    in_vmem = pl.BlockSpec(memory_space=pltpu.VMEM)
    in_hbm = pl.BlockSpec(memory_space=pltpu.HBM)
    piece = pltpu.VMEM(quarter, jnp.bfloat16)
    few = pltpu.CompilerParams(vmem_limit_bytes=MIB)
    latent, cotangent = latent.transpose(1, 2, 0, 3), cotangent.transpose(1, 2, 0, 3)

    to_both, to_lat, to_lon = pl.pallas_call(
        cut_kernel,
        in_specs=[in_hbm] * 2,
        out_specs=[in_vmem] * 3,
        out_shape=[piece] * 3,
        scratch_shapes=[pltpu.SemaphoreType.DMA((3, 2))],
        compiler_params=few,
        name="cut",
    )(stay(latent), stay(cotangent))

    from_both = neighbour(to_both, LAT_STEP, LON_STEP)
    from_lat = neighbour(to_lat, LAT_STEP, 0)
    from_lon = neighbour(to_lon, 0, LON_STEP)

    own, *parameters = pl.pallas_call(
        fetch_kernel,
        in_specs=[in_hbm] * 5,
        out_specs=[in_vmem] * 6,
        out_shape=[
            piece,
            pltpu.VMEM((1, features), jnp.float32),
            pltpu.VMEM(qkv_weight.shape, jnp.bfloat16),
            pltpu.VMEM(out_weight.shape, jnp.bfloat16),
            pltpu.VMEM(qkv_weight.shape[::-1], jnp.bfloat16),
            pltpu.VMEM(out_weight.shape[::-1], jnp.bfloat16),
        ],
        scratch_shapes=[pltpu.SemaphoreType.DMA((5,))],
        compiler_params=few,
        cost_estimate=pl.CostEstimate(flops=0, bytes_accessed=4 * MIB, transcendentals=0),
        name="fetch",
    )(*map(stay, (latent, cotangent, norm_gain.reshape(1, features), qkv_weight, out_weight)))

    to_both, to_lat, to_lon, own = pl.pallas_call(
        window_kernel,
        in_specs=[in_vmem] * 9,
        out_specs=[in_vmem] * 4,
        out_shape=[piece] * 4,
        scratch_shapes=[
            pltpu.VMEM((window, features), jnp.float32),
            pltpu.VMEM((window, features), jnp.float32),
            pltpu.VMEM(packed, jnp.float32),
            pltpu.VMEM(packed, jnp.bfloat16),
            pltpu.VMEM(packed, jnp.float32),
            pltpu.VMEM((HEADS // GROUP, GROUP * window, features * GROUP // HEADS), jnp.bfloat16),
            pltpu.VMEM((window, 3 * features), jnp.bfloat16),
            pltpu.VMEM((window, features), jnp.bfloat16),
            pltpu.VMEM((window, 3 * features), jnp.bfloat16),
        ],
        compiler_params=pltpu.CompilerParams(vmem_limit_bytes=12 * MIB),
        name="window",
    )(from_both, from_lat, from_lon, own, *parameters)

    from_both = neighbour(to_both, -LAT_STEP, -LON_STEP)
    from_lat = neighbour(to_lat, -LAT_STEP, 0)
    from_lon = neighbour(to_lon, 0, -LON_STEP)

    updated, latent_grad = pl.pallas_call(
        join_kernel,
        in_specs=[in_vmem] * 4,
        out_specs=[in_hbm] * 2,
        out_shape=[jax.ShapeDtypeStruct((rows, cols, levels, features), jnp.bfloat16)] * 2,
        scratch_shapes=[pltpu.SemaphoreType.DMA((4, 2))],
        compiler_params=few,
        name="join",
    )(from_both, from_lat, from_lon, own)
    return (updated.transpose(2, 0, 1, 3), latent_grad.transpose(2, 0, 1, 3))


def solution(mesh):
    placed = (P(None, "lat", "lon", None), P(None, "lat", "lon", None), P(), P(), P())
    return jax.shard_map(
        body,
        mesh=mesh,
        in_specs=placed,
        out_specs=(P(None, "lat", "lon", None), P(None, "lat", "lon", None)),
        check_vma=False,
    )
```

```python
import math

import jax
import jax.numpy as jnp
from jax import lax
from jax.experimental import pallas as pl
from jax.experimental.pallas import tpu as pltpu
from jax.sharding import PartitionSpec as P

HEADS = 8
WLAT = 12
WLON = 6
SLAT = 6
SLON = 3
GROUP = 4

MIB = 1 << 20
NORM_EPS = 1e-05
MASK_FILL = -1000000000.0

LAT_STEP = 1
LON_STEP = 1


def neighbour(piece, lat_by, lon_by):
    lats, lons = lax.axis_size("lat"), lax.axis_size("lon")
    pairs = [
        (i * lons + j, (i + lat_by) % lats * lons + (j + lon_by) % lons)
        for i in range(lats)
        for j in range(lons)
    ]
    return lax.ppermute(piece, ("lat", "lon"), pairs)


def corners(rows, cols):
    early_rows, late_rows = pl.ds(0, SLAT), pl.ds(SLAT, rows - SLAT)
    early_cols, late_cols = pl.ds(0, SLON), pl.ds(SLON, cols - SLON)
    go_rows, stay_rows = (early_rows, late_rows) if LAT_STEP < 0 else (late_rows, early_rows)
    go_cols, stay_cols = (early_cols, late_cols) if LON_STEP < 0 else (late_cols, early_cols)
    return (
        (go_rows, go_cols), (go_rows, stay_cols), (stay_rows, go_cols), (stay_rows, stay_cols)
    )


def stay(x):
    return pltpu.with_memory_space_constraint(x, pltpu.HBM)


def cut_kernel(latent, cotangent, *rest):
    pieces, sems = rest[:3], rest[3]
    copies = []
    for k, (rows, cols) in enumerate(corners(*latent.shape[:2])[:3]):
        for f, field in enumerate((latent, cotangent)):
            copies.append(
                pltpu.make_async_copy(field.at[rows, cols], pieces[k].at[f], sems.at[k, f])
            )
    for copy in copies:
        copy.start()
    for copy in copies:
        copy.wait()


def fetch_kernel(
    latent, cotangent, gain, qkv, out, own, gain_to, qkv_to, out_to, qkv_turned, out_turned, sems
):
    rows, cols = corners(*latent.shape[:2])[3]
    copies = [
        pltpu.make_async_copy(qkv, qkv_to, sems.at[0]),
        pltpu.make_async_copy(out, out_to, sems.at[1]),
        pltpu.make_async_copy(gain, gain_to, sems.at[2]),
        pltpu.make_async_copy(latent.at[rows, cols], own.at[0], sems.at[3]),
        pltpu.make_async_copy(cotangent.at[rows, cols], own.at[1], sems.at[4]),
    ]
    for copy in copies:
        copy.start()
    copies[1].wait()
    out_turned[...] = out_to[...].T
    copies[0].wait()
    qkv_turned[...] = qkv_to[...].T
    for copy in copies[2:]:
        copy.wait()


def join_kernel(*refs):
    quarters, outs, sems = (*refs[2::-1], refs[3]), refs[4:6], refs[6]
    copies = []
    for k, (rows, cols) in enumerate(corners(*outs[0].shape[:2])):
        for f, field in enumerate(outs):
            copies.append(
                pltpu.make_async_copy(quarters[k].at[f], field.at[rows, cols], sems.at[k, f])
            )
    for copy in copies:
        copy.start()
    for copy in copies:
        copy.wait()


def across(a, b):
    return lax.dot_general(a, b, (((1,), (1,)), ((), ())), preferred_element_type=jnp.float32)


def down(a, b):
    return lax.dot_general(a, b, (((0,), (0,)), ((), ())), preferred_element_type=jnp.float32)


def matmul(a, b):
    return jnp.dot(a, b, preferred_element_type=jnp.float32)


def window_kernel(
    ahead_both, ahead_lat, ahead_lon, own, gain_ref, qkv_ref, out_ref, qkv_turned, out_turned,
    both_out, lat_out, lon_out, own_out,
    tokens, cots, scores_ref, low_ref, slopes_ref, wide_query, proj_ref, mixed_ref, grad_ref,
):
    quarters = (ahead_both, ahead_lat, ahead_lon, own)
    results = (both_out, lat_out, lon_out, own_out)
    _, rows, cols, levels, features = own.shape
    quarter = rows * cols * levels
    window = 4 * quarter
    head_dim = features // HEADS
    scale = 1.0 / math.sqrt(head_dim)

    for k, ref in enumerate(quarters):
        for f, into in enumerate((tokens, cots)):
            for r in range(rows):
                for c in range(cols):
                    at = k * quarter + (r * cols + c) * levels
                    into[at : at + levels, :] = ref[f, r, c].astype(jnp.float32)

    proj = matmul(tokens[...].astype(jnp.bfloat16), qkv_ref[...]).astype(jnp.bfloat16)
    proj_ref[:, features:] = proj[:, features:]
    proj_ref[:, :features] = proj[:, :features] * jnp.asarray(scale, jnp.bfloat16)

    last = lax.axis_index("lat") == (lax.axis_size("lat") - 1 if LAT_STEP < 0 else 0)
    wide = GROUP * head_dim
    packed = GROUP * window
    key_row = lax.broadcasted_iota(jnp.int32, (window, packed), 0)
    query_row = lax.rem(lax.broadcasted_iota(jnp.int32, (window, packed), 1), window)
    fill = jnp.where(last, MASK_FILL, 0.0).astype(jnp.float32)
    bias = jnp.where((key_row < 2 * quarter) != (query_row < 2 * quarter), fill, 0.0)
    lane = lax.broadcasted_iota(jnp.int32, (1, wide), 1)
    only = [(lane // head_dim == e).astype(jnp.float32).astype(jnp.bfloat16) for e in range(GROUP)]
    mine = [lax.broadcasted_iota(jnp.int32, (window, wide), 1) < head_dim * e for e in range(1, GROUP)]

    def part(ref, which, group):
        at = which * features + wide * group
        return ref[:, at : at + wide]

    def fanned(x):
        return jnp.concatenate([x * only[e] for e in range(GROUP)], axis=0)

    def gathered(x):
        out = x[(GROUP - 1) * window :]
        for e in range(GROUP - 2, -1, -1):
            out = jnp.where(mine[e], x[e * window : (e + 1) * window], out)
        return out

    for group in range(HEADS // GROUP):
        wide_query[group] = fanned(part(proj_ref, 0, group))
        scores_ref[group] = across(part(proj_ref, 1, group), wide_query[group])

    for group in range(HEADS // GROUP):
        scores = scores_ref[group] + bias
        grown = jnp.exp(scores - jnp.max(scores, axis=0, keepdims=True))
        probs = grown * (1.0 / jnp.sum(grown, axis=0, keepdims=True))
        scores_ref[group] = probs
        low_ref[group] = probs.astype(jnp.bfloat16)

    for group in range(HEADS // GROUP):
        at = wide * group
        mixed = gathered(down(low_ref[group], part(proj_ref, 2, group)))
        mixed_ref[:, at : at + wide] = mixed.astype(jnp.bfloat16)

    branch = matmul(mixed_ref[...], out_ref[...]).astype(jnp.bfloat16).astype(jnp.float32)
    gain = gain_ref[...]
    upstream = gain * cots[...]
    centre_up = jnp.mean(upstream, axis=-1, keepdims=True)
    centred = branch - jnp.mean(branch, axis=-1, keepdims=True)
    spread = jnp.mean(centred * centred, axis=-1, keepdims=True)
    along = jnp.mean(upstream * centred, axis=-1, keepdims=True)
    inverse = lax.rsqrt(spread + NORM_EPS)
    normed = centred * inverse
    tokens[...] = tokens[...] + gain * normed
    grad_branch = (inverse * (upstream - centre_up - normed * (along * inverse))).astype(jnp.bfloat16)
    mixed_ref[...] = matmul(grad_branch, out_turned[...]).astype(jnp.bfloat16)

    def put(which, group, x):
        at = which * features + wide * group
        grad_ref[:, at : at + wide] = x.astype(jnp.bfloat16)

    for group in range(HEADS // GROUP):
        grad_mixed = fanned(part(mixed_ref, 0, group))
        slopes_ref[group] = across(part(proj_ref, 2, group), grad_mixed)
        put(2, group, matmul(low_ref[group], grad_mixed))

    for group in range(HEADS // GROUP):
        probs, grad_probs = scores_ref[group], slopes_ref[group]
        along = jnp.sum(grad_probs * probs, axis=0, keepdims=True)
        low_ref[group] = (probs * (grad_probs - along)).astype(jnp.bfloat16)

    for group in range(HEADS // GROUP):
        put(0, group, gathered(down(low_ref[group], part(proj_ref, 1, group))) * scale)
        put(1, group, matmul(low_ref[group], wide_query[group]))

    grad_tokens = matmul(grad_ref[...], qkv_turned[...]).astype(jnp.bfloat16).astype(jnp.float32)
    cots[...] = cots[...] + grad_tokens

    for k, ref in enumerate(results):
        for f, source in enumerate((tokens, cots)):
            for r in range(rows):
                for c in range(cols):
                    at = k * quarter + (r * cols + c) * levels
                    ref[f, r, c] = source[at : at + levels, :].astype(jnp.bfloat16)


def body(latent, cotangent, norm_gain, qkv_weight, out_weight):
    levels, rows, cols, features = latent.shape
    assert (rows, cols) == (WLAT, WLON) and (2 * SLAT, 2 * SLON) == (WLAT, WLON)
    window = levels * rows * cols
    quarter = (2, SLAT, SLON, levels, features)
    packed = (HEADS // GROUP, window, GROUP * window)
    in_vmem = pl.BlockSpec(memory_space=pltpu.VMEM)
    in_hbm = pl.BlockSpec(memory_space=pltpu.HBM)
    piece = pltpu.VMEM(quarter, jnp.bfloat16)
    few = pltpu.CompilerParams(vmem_limit_bytes=MIB)
    latent, cotangent = latent.transpose(1, 2, 0, 3), cotangent.transpose(1, 2, 0, 3)

    to_both, to_lat, to_lon = pl.pallas_call(
        cut_kernel,
        in_specs=[in_hbm] * 2,
        out_specs=[in_vmem] * 3,
        out_shape=[piece] * 3,
        scratch_shapes=[pltpu.SemaphoreType.DMA((3, 2))],
        compiler_params=few,
        name="cut",
    )(stay(latent), stay(cotangent))

    from_both = neighbour(to_both, LAT_STEP, LON_STEP)
    from_lat = neighbour(to_lat, LAT_STEP, 0)
    from_lon = neighbour(to_lon, 0, LON_STEP)

    own, *parameters = pl.pallas_call(
        fetch_kernel,
        in_specs=[in_hbm] * 5,
        out_specs=[in_vmem] * 6,
        out_shape=[
            piece,
            pltpu.VMEM((1, features), jnp.float32),
            pltpu.VMEM(qkv_weight.shape, jnp.bfloat16),
            pltpu.VMEM(out_weight.shape, jnp.bfloat16),
            pltpu.VMEM(qkv_weight.shape[::-1], jnp.bfloat16),
            pltpu.VMEM(out_weight.shape[::-1], jnp.bfloat16),
        ],
        scratch_shapes=[pltpu.SemaphoreType.DMA((5,))],
        compiler_params=few,
        cost_estimate=pl.CostEstimate(flops=0, bytes_accessed=4 * MIB, transcendentals=0),
        name="fetch",
    )(*map(stay, (latent, cotangent, norm_gain.reshape(1, features), qkv_weight, out_weight)))

    to_both, to_lat, to_lon, own = pl.pallas_call(
        window_kernel,
        in_specs=[in_vmem] * 9,
        out_specs=[in_vmem] * 4,
        out_shape=[piece] * 4,
        scratch_shapes=[
            pltpu.VMEM((window, features), jnp.float32),
            pltpu.VMEM((window, features), jnp.float32),
            pltpu.VMEM(packed, jnp.float32),
            pltpu.VMEM(packed, jnp.bfloat16),
            pltpu.VMEM(packed, jnp.float32),
            pltpu.VMEM((HEADS // GROUP, GROUP * window, features * GROUP // HEADS), jnp.bfloat16),
            pltpu.VMEM((window, 3 * features), jnp.bfloat16),
            pltpu.VMEM((window, features), jnp.bfloat16),
            pltpu.VMEM((window, 3 * features), jnp.bfloat16),
        ],
        compiler_params=pltpu.CompilerParams(vmem_limit_bytes=12 * MIB),
        name="window",
    )(from_both, from_lat, from_lon, own, *parameters)

    from_both = neighbour(to_both, -LAT_STEP, -LON_STEP)
    from_lat = neighbour(to_lat, -LAT_STEP, 0)
    from_lon = neighbour(to_lon, 0, -LON_STEP)

    updated, latent_grad = pl.pallas_call(
        join_kernel,
        in_specs=[in_vmem] * 4,
        out_specs=[in_hbm] * 2,
        out_shape=[jax.ShapeDtypeStruct((rows, cols, levels, features), jnp.bfloat16)] * 2,
        scratch_shapes=[pltpu.SemaphoreType.DMA((4, 2))],
        compiler_params=few,
        name="join",
    )(from_lon, from_lat, from_both, own)
    return (updated.transpose(2, 0, 1, 3), latent_grad.transpose(2, 0, 1, 3))


def solution(mesh):
    placed = (P(None, "lat", "lon", None), P(None, "lat", "lon", None), P(), P(), P())
    return jax.shard_map(
        body,
        mesh=mesh,
        in_specs=placed,
        out_specs=(P(None, "lat", "lon", None), P(None, "lat", "lon", None)),
        check_vma=False,
    )
```

```python
import math

import jax
import jax.numpy as jnp
from jax import lax
from jax.experimental import pallas as pl
from jax.experimental.pallas import tpu as pltpu
from jax.sharding import PartitionSpec as P

HEADS = 8
WLAT = 12
WLON = 6
SLAT = 6
SLON = 3
GROUP = 4
STRIP = 256

MIB = 1 << 20
NORM_EPS = 1e-05
MASK_FILL = -1000000000.0

LAT_STEP = 1
LON_STEP = -1


def neighbour(piece, lat_by, lon_by):
    lats, lons = lax.axis_size("lat"), lax.axis_size("lon")
    pairs = [
        (i * lons + j, (i + lat_by) % lats * lons + (j + lon_by) % lons)
        for i in range(lats)
        for j in range(lons)
    ]
    return lax.ppermute(piece, ("lat", "lon"), pairs)


def corners(rows, cols):
    early_rows, late_rows = pl.ds(0, SLAT), pl.ds(SLAT, rows - SLAT)
    early_cols, late_cols = pl.ds(0, SLON), pl.ds(SLON, cols - SLON)
    go_rows, stay_rows = (early_rows, late_rows) if LAT_STEP < 0 else (late_rows, early_rows)
    go_cols, stay_cols = (early_cols, late_cols) if LON_STEP < 0 else (late_cols, early_cols)
    return (
        (go_rows, go_cols), (go_rows, stay_cols), (stay_rows, go_cols), (stay_rows, stay_cols)
    )


def stay(x):
    return pltpu.with_memory_space_constraint(x, pltpu.HBM)


def cut_kernel(latent, cotangent, *rest):
    pieces, sems = rest[:3], rest[3]
    copies = []
    for k, (rows, cols) in enumerate(corners(*latent.shape[:2])[:3]):
        for f, field in enumerate((latent, cotangent)):
            copies.append(
                pltpu.make_async_copy(field.at[rows, cols], pieces[k].at[f], sems.at[k, f])
            )
    for copy in copies:
        copy.start()
    for copy in copies:
        copy.wait()


def fetch_kernel(
    latent, cotangent, gain, qkv, out, own, gain_to, qkv_to, out_to, qkv_turned, out_turned, sems
):
    rows, cols = corners(*latent.shape[:2])[3]
    pieces = []
    for source, into, turned in ((out, out_to, out_turned), (qkv, qkv_to, qkv_turned)):
        for at in range(0, source.shape[0], STRIP):
            pieces.append((source, into, turned, pl.ds(at, STRIP)))
    strips = [
        pltpu.make_async_copy(source.at[at], into.at[at], sems.at[k])
        for k, (source, into, _, at) in enumerate(pieces)
    ]
    others = [
        pltpu.make_async_copy(gain, gain_to, sems.at[len(strips)]),
        pltpu.make_async_copy(latent.at[rows, cols], own.at[0], sems.at[len(strips) + 1]),
        pltpu.make_async_copy(cotangent.at[rows, cols], own.at[1], sems.at[len(strips) + 2]),
    ]
    for copy in strips + others:
        copy.start()
    for copy, (_, into, turned, at) in zip(strips, pieces):
        copy.wait()
        turned[:, at] = into[at].T
    for copy in others:
        copy.wait()


def join_kernel(*refs):
    quarters, outs, sems = (refs[0], refs[2], refs[1], refs[3]), refs[4:6], refs[6]
    copies = []
    for k, (rows, cols) in enumerate(corners(*outs[0].shape[:2])):
        for f, field in enumerate(outs):
            copies.append(
                pltpu.make_async_copy(quarters[k].at[f], field.at[rows, cols], sems.at[k, f])
            )
    for copy in copies:
        copy.start()
    for copy in copies:
        copy.wait()


def across(a, b):
    return lax.dot_general(a, b, (((1,), (1,)), ((), ())), preferred_element_type=jnp.float32)


def down(a, b):
    return lax.dot_general(a, b, (((0,), (0,)), ((), ())), preferred_element_type=jnp.float32)


def matmul(a, b):
    return jnp.dot(a, b, preferred_element_type=jnp.float32)


def window_kernel(
    ahead_lat, ahead_both, ahead_lon, own, gain_ref, qkv_ref, out_ref, qkv_turned, out_turned,
    both_out, lat_out, lon_out, own_out,
    tokens, cots, scores_ref, low_ref, slopes_ref, wide_query, proj_ref, mixed_ref, grad_ref,
):
    quarters = (ahead_both, ahead_lat, ahead_lon, own)
    results = (both_out, lat_out, lon_out, own_out)
    _, rows, cols, levels, features = own.shape
    quarter = rows * cols * levels
    window = 4 * quarter
    head_dim = features // HEADS
    scale = 1.0 / math.sqrt(head_dim)

    for k, ref in enumerate(quarters):
        for f, into in enumerate((tokens, cots)):
            for r in range(rows):
                for c in range(cols):
                    at = k * quarter + (r * cols + c) * levels
                    into[at : at + levels, :] = ref[f, r, c].astype(jnp.float32)

    proj = matmul(tokens[...].astype(jnp.bfloat16), qkv_ref[...]).astype(jnp.bfloat16)
    proj_ref[:, features:] = proj[:, features:]
    proj_ref[:, :features] = proj[:, :features] * jnp.asarray(scale, jnp.bfloat16)

    last = lax.axis_index("lat") == (lax.axis_size("lat") - 1 if LAT_STEP < 0 else 0)
    wide = GROUP * head_dim
    packed = GROUP * window
    key_row = lax.broadcasted_iota(jnp.int32, (window, packed), 0)
    query_row = lax.rem(lax.broadcasted_iota(jnp.int32, (window, packed), 1), window)
    fill = jnp.where(last, MASK_FILL, 0.0).astype(jnp.float32)
    bias = jnp.where((key_row < 2 * quarter) != (query_row < 2 * quarter), fill, 0.0)
    lane = lax.broadcasted_iota(jnp.int32, (1, wide), 1)
    only = [(lane // head_dim == e).astype(jnp.float32).astype(jnp.bfloat16) for e in range(GROUP)]
    mine = [lax.broadcasted_iota(jnp.int32, (window, wide), 1) < head_dim * e for e in range(1, GROUP)]

    def part(ref, which, group):
        at = which * features + wide * group
        return ref[:, at : at + wide]

    def fanned(x):
        return jnp.concatenate([x * only[e] for e in range(GROUP)], axis=0)

    def gathered(x):
        out = x[(GROUP - 1) * window :]
        for e in range(GROUP - 2, -1, -1):
            out = jnp.where(mine[e], x[e * window : (e + 1) * window], out)
        return out

    for group in range(HEADS // GROUP):
        wide_query[group] = fanned(part(proj_ref, 0, group))
        scores_ref[group] = across(part(proj_ref, 1, group), wide_query[group])

    for group in range(HEADS // GROUP):
        scores = scores_ref[group] + bias
        grown = jnp.exp(scores - jnp.max(scores, axis=0, keepdims=True))
        probs = grown * (1.0 / jnp.sum(grown, axis=0, keepdims=True))
        scores_ref[group] = probs
        low_ref[group] = probs.astype(jnp.bfloat16)

    for group in range(HEADS // GROUP):
        at = wide * group
        mixed = gathered(down(low_ref[group], part(proj_ref, 2, group)))
        mixed_ref[:, at : at + wide] = mixed.astype(jnp.bfloat16)

    branch = matmul(mixed_ref[...], out_ref[...]).astype(jnp.bfloat16).astype(jnp.float32)
    gain = gain_ref[...]
    upstream = gain * cots[...]
    centre_up = jnp.mean(upstream, axis=-1, keepdims=True)
    centred = branch - jnp.mean(branch, axis=-1, keepdims=True)
    spread = jnp.mean(centred * centred, axis=-1, keepdims=True)
    along = jnp.mean(upstream * centred, axis=-1, keepdims=True)
    inverse = lax.rsqrt(spread + NORM_EPS)
    normed = centred * inverse
    tokens[...] = tokens[...] + gain * normed
    grad_branch = (inverse * (upstream - centre_up - normed * (along * inverse))).astype(jnp.bfloat16)
    mixed_ref[...] = matmul(grad_branch, out_turned[...]).astype(jnp.bfloat16)

    def put(which, group, x):
        at = which * features + wide * group
        grad_ref[:, at : at + wide] = x.astype(jnp.bfloat16)

    for group in range(HEADS // GROUP):
        grad_mixed = fanned(part(mixed_ref, 0, group))
        slopes_ref[group] = across(part(proj_ref, 2, group), grad_mixed)
        put(2, group, matmul(low_ref[group], grad_mixed))

    for group in range(HEADS // GROUP):
        probs, grad_probs = scores_ref[group], slopes_ref[group]
        along = jnp.sum(grad_probs * probs, axis=0, keepdims=True)
        low_ref[group] = (probs * (grad_probs - along)).astype(jnp.bfloat16)

    for group in range(HEADS // GROUP):
        put(0, group, gathered(down(low_ref[group], part(proj_ref, 1, group))) * scale)
        put(1, group, matmul(low_ref[group], wide_query[group]))

    grad_tokens = matmul(grad_ref[...], qkv_turned[...]).astype(jnp.bfloat16).astype(jnp.float32)
    cots[...] = cots[...] + grad_tokens

    for k, ref in enumerate(results):
        for f, source in enumerate((tokens, cots)):
            for r in range(rows):
                for c in range(cols):
                    at = k * quarter + (r * cols + c) * levels
                    ref[f, r, c] = source[at : at + levels, :].astype(jnp.bfloat16)


def body(latent, cotangent, norm_gain, qkv_weight, out_weight):
    levels, rows, cols, features = latent.shape
    assert (rows, cols) == (WLAT, WLON) and (2 * SLAT, 2 * SLON) == (WLAT, WLON)
    window = levels * rows * cols
    quarter = (2, SLAT, SLON, levels, features)
    packed = (HEADS // GROUP, window, GROUP * window)
    in_vmem = pl.BlockSpec(memory_space=pltpu.VMEM)
    in_hbm = pl.BlockSpec(memory_space=pltpu.HBM)
    piece = pltpu.VMEM(quarter, jnp.bfloat16)
    few = pltpu.CompilerParams(vmem_limit_bytes=MIB)
    latent, cotangent = latent.transpose(1, 2, 0, 3), cotangent.transpose(1, 2, 0, 3)

    to_both, to_lat, to_lon = pl.pallas_call(
        cut_kernel,
        in_specs=[in_hbm] * 2,
        out_specs=[in_vmem] * 3,
        out_shape=[piece] * 3,
        scratch_shapes=[pltpu.SemaphoreType.DMA((3, 2))],
        compiler_params=few,
        name="cut",
    )(stay(latent), stay(cotangent))

    from_both = neighbour(to_both, LAT_STEP, LON_STEP)
    from_lat = neighbour(to_lat, LAT_STEP, 0)
    from_lon = neighbour(to_lon, 0, LON_STEP)

    own, *parameters = pl.pallas_call(
        fetch_kernel,
        in_specs=[in_hbm] * 5,
        out_specs=[in_vmem] * 6,
        out_shape=[
            piece,
            pltpu.VMEM((1, features), jnp.float32),
            pltpu.VMEM(qkv_weight.shape, jnp.bfloat16),
            pltpu.VMEM(out_weight.shape, jnp.bfloat16),
            pltpu.VMEM(qkv_weight.shape[::-1], jnp.bfloat16),
            pltpu.VMEM(out_weight.shape[::-1], jnp.bfloat16),
        ],
        scratch_shapes=[pltpu.SemaphoreType.DMA((2 * features // STRIP + 3,))],
        compiler_params=few,
        cost_estimate=pl.CostEstimate(flops=0, bytes_accessed=4 * MIB, transcendentals=0),
        name="fetch",
    )(*map(stay, (latent, cotangent, norm_gain.reshape(1, features), qkv_weight, out_weight)))

    to_both, to_lat, to_lon, own = pl.pallas_call(
        window_kernel,
        in_specs=[in_vmem] * 9,
        out_specs=[in_vmem] * 4,
        out_shape=[piece] * 4,
        scratch_shapes=[
            pltpu.VMEM((window, features), jnp.float32),
            pltpu.VMEM((window, features), jnp.float32),
            pltpu.VMEM(packed, jnp.float32),
            pltpu.VMEM(packed, jnp.bfloat16),
            pltpu.VMEM(packed, jnp.float32),
            pltpu.VMEM((HEADS // GROUP, GROUP * window, features * GROUP // HEADS), jnp.bfloat16),
            pltpu.VMEM((window, 3 * features), jnp.bfloat16),
            pltpu.VMEM((window, features), jnp.bfloat16),
            pltpu.VMEM((window, 3 * features), jnp.bfloat16),
        ],
        compiler_params=pltpu.CompilerParams(vmem_limit_bytes=12 * MIB),
        name="window",
    )(from_lat, from_both, from_lon, own, *parameters)

    from_both = neighbour(to_both, -LAT_STEP, -LON_STEP)
    from_lat = neighbour(to_lat, -LAT_STEP, 0)
    from_lon = neighbour(to_lon, 0, -LON_STEP)

    updated, latent_grad = pl.pallas_call(
        join_kernel,
        in_specs=[in_vmem] * 4,
        out_specs=[in_hbm] * 2,
        out_shape=[jax.ShapeDtypeStruct((rows, cols, levels, features), jnp.bfloat16)] * 2,
        scratch_shapes=[pltpu.SemaphoreType.DMA((4, 2))],
        compiler_params=few,
        name="join",
    )(from_both, from_lon, from_lat, own)
    return (updated.transpose(2, 0, 1, 3), latent_grad.transpose(2, 0, 1, 3))


def solution(mesh):
    placed = (P(None, "lat", "lon", None), P(None, "lat", "lon", None), P(), P(), P())
    return jax.shard_map(
        body,
        mesh=mesh,
        in_specs=placed,
        out_specs=(P(None, "lat", "lon", None), P(None, "lat", "lon", None)),
        check_vma=False,
    )
```

```python
import functools
import math

import jax
import jax.numpy as jnp
from jax import lax
from jax.experimental import pallas as pl
from jax.experimental.pallas import tpu as pltpu
from jax.sharding import PartitionSpec as P

HEADS = 8
WLAT = 12
WLON = 6
SLAT = 6
SLON = 3
GROUP = 4
STRIP = 256

MIB = 1 << 20
NORM_EPS = 1e-05
MASK_FILL = -1000000000.0

LAT_STEP = 1
LON_STEP = -1


def neighbour(piece, lat_by, lon_by):
    lats, lons = lax.axis_size("lat"), lax.axis_size("lon")
    pairs = [
        (i * lons + j, (i + lat_by) % lats * lons + (j + lon_by) % lons)
        for i in range(lats)
        for j in range(lons)
    ]
    return lax.ppermute(piece, ("lat", "lon"), pairs)


def corners(rows, cols):
    early_rows, late_rows = pl.ds(0, SLAT), pl.ds(SLAT, rows - SLAT)
    early_cols, late_cols = pl.ds(0, SLON), pl.ds(SLON, cols - SLON)
    go_rows, stay_rows = (early_rows, late_rows) if LAT_STEP < 0 else (late_rows, early_rows)
    go_cols, stay_cols = (early_cols, late_cols) if LON_STEP < 0 else (late_cols, early_cols)
    return (
        (go_rows, go_cols), (go_rows, stay_cols), (stay_rows, go_cols), (stay_rows, stay_cols)
    )


def stay(x):
    return pltpu.with_memory_space_constraint(x, pltpu.HBM)


def cut_kernel(latent, cotangent, *rest):
    pieces, sems = rest[:3], rest[3]
    copies = []
    for k, (rows, cols) in enumerate(corners(*latent.shape[:2])[:3]):
        for f, field in enumerate((latent, cotangent)):
            copies.append(
                pltpu.make_async_copy(field.at[rows, cols], pieces[k].at[f], sems.at[k, f])
            )
    for copy in copies:
        copy.start()
    for copy in copies:
        copy.wait()


def fetch_kernel(
    latent, cotangent, gain, qkv, out, own, gain_to, qkv_to, out_to, qkv_turned, out_turned, sems
):
    rows, cols = corners(*latent.shape[:2])[3]
    width = out.shape[1]
    scale = 1.0 / math.sqrt(width // HEADS)
    pieces = []
    for source, into, turned in ((out, out_to, out_turned), (qkv, qkv_to, qkv_turned)):
        for at in range(0, source.shape[0], STRIP):
            pieces.append((source, into, turned, pl.ds(at, STRIP)))
    strips = [
        pltpu.make_async_copy(source.at[at], into.at[at], sems.at[k])
        for k, (source, into, _, at) in enumerate(pieces)
    ]
    others = [
        pltpu.make_async_copy(gain, gain_to, sems.at[len(strips)]),
        pltpu.make_async_copy(latent.at[rows, cols], own.at[0], sems.at[len(strips) + 1]),
        pltpu.make_async_copy(cotangent.at[rows, cols], own.at[1], sems.at[len(strips) + 2]),
    ]
    for copy in strips + others:
        copy.start()
    for copy, (_, into, turned, at) in zip(strips, pieces):
        copy.wait()
        if into is qkv_to:
            into[at, :width] = into[at, :width] * jnp.asarray(scale, jnp.bfloat16)
        turned[:, at] = into[at].T
    for copy in others:
        copy.wait()


def join_kernel(which, *refs):
    quarters, outs, sems = refs[: len(which)], refs[-3:-1], refs[-1]
    places = corners(*outs[0].shape[:2])
    copies = []
    for k, place in enumerate(which):
        for f, field in enumerate(outs):
            rows, cols = places[place]
            copies.append(
                pltpu.make_async_copy(quarters[k].at[f], field.at[rows, cols], sems.at[k, f])
            )
    for copy in copies:
        copy.start()
    for copy in copies:
        copy.wait()


def across(a, b):
    return lax.dot_general(a, b, (((1,), (1,)), ((), ())), preferred_element_type=jnp.float32)


def down(a, b):
    return lax.dot_general(a, b, (((0,), (0,)), ((), ())), preferred_element_type=jnp.float32)


def matmul(a, b):
    return jnp.dot(a, b, preferred_element_type=jnp.float32)


def window_kernel(
    ahead_lat, ahead_both, ahead_lon, own, gain_ref, qkv_ref, out_ref, qkv_turned, out_turned,
    both_out, lat_out, lon_out, own_out,
    tokens, cots, scores_ref, low_ref, slopes_ref, wide_query, proj_ref, mixed_ref, grad_ref,
):
    quarters = (ahead_both, ahead_lat, ahead_lon, own)
    results = (both_out, lat_out, lon_out, own_out)
    _, rows, cols, levels, features = own.shape
    quarter = rows * cols * levels
    window = 4 * quarter
    head_dim = features // HEADS

    for k, ref in enumerate(quarters):
        for f, into in enumerate((tokens, cots)):
            for r in range(rows):
                for c in range(cols):
                    at = k * quarter + (r * cols + c) * levels
                    into[at : at + levels, :] = ref[f, r, c].astype(jnp.float32)

    proj_ref[...] = matmul(tokens[...].astype(jnp.bfloat16), qkv_ref[...]).astype(jnp.bfloat16)

    last = lax.axis_index("lat") == (lax.axis_size("lat") - 1 if LAT_STEP < 0 else 0)
    wide = GROUP * head_dim
    packed = GROUP * window
    key_row = lax.broadcasted_iota(jnp.int32, (window, packed), 0)
    query_row = lax.rem(lax.broadcasted_iota(jnp.int32, (window, packed), 1), window)
    fill = jnp.where(last, MASK_FILL, 0.0).astype(jnp.float32)
    bias = jnp.where((key_row < 2 * quarter) != (query_row < 2 * quarter), fill, 0.0)
    lane = lax.broadcasted_iota(jnp.int32, (1, wide), 1)
    only = [(lane // head_dim == e).astype(jnp.float32).astype(jnp.bfloat16) for e in range(GROUP)]
    first = lax.broadcasted_iota(jnp.int32, (window, 2 * head_dim), 1) < head_dim

    def part(ref, which, group):
        at = which * features + wide * group
        return ref[:, at : at + wide]

    def fanned(x):
        return jnp.concatenate([x * only[e] for e in range(GROUP)], axis=0)

    def gathered(packed_rows, x):
        rows_first, parts = packed_rows.T, []
        for pair in range(GROUP // 2):
            lanes = slice(2 * head_dim * pair, 2 * head_dim * (pair + 1))
            both = matmul(rows_first[2 * window * pair : 2 * window * (pair + 1)], x[:, lanes])
            parts.append(jnp.where(first, both[:window], both[window:]))
        return jnp.concatenate(parts, axis=1)

    for group in range(HEADS // GROUP):
        wide_query[group] = fanned(part(proj_ref, 0, group))
        scores_ref[group] = across(part(proj_ref, 1, group), wide_query[group])

    for group in range(HEADS // GROUP):
        scores = scores_ref[group] + bias
        grown = jnp.exp(scores - jnp.max(scores, axis=0, keepdims=True))
        probs = grown * (1.0 / jnp.sum(grown, axis=0, keepdims=True))
        scores_ref[group] = probs
        low_ref[group] = probs.astype(jnp.bfloat16)

    for group in range(HEADS // GROUP):
        at = wide * group
        mixed = gathered(low_ref[group], part(proj_ref, 2, group))
        mixed_ref[:, at : at + wide] = mixed.astype(jnp.bfloat16)

    branch = matmul(mixed_ref[...], out_ref[...]).astype(jnp.bfloat16).astype(jnp.float32)
    gain = gain_ref[...]
    upstream = gain * cots[...]
    centre_up = jnp.mean(upstream, axis=-1, keepdims=True)
    centred = branch - jnp.mean(branch, axis=-1, keepdims=True)
    spread = jnp.mean(centred * centred, axis=-1, keepdims=True)
    along = jnp.mean(upstream * centred, axis=-1, keepdims=True)
    inverse = lax.rsqrt(spread + NORM_EPS)
    normed = centred * inverse
    tokens[...] = tokens[...] + gain * normed
    grad_branch = (inverse * (upstream - centre_up - normed * (along * inverse))).astype(jnp.bfloat16)
    mixed_ref[...] = matmul(grad_branch, out_turned[...]).astype(jnp.bfloat16)

    def put(which, group, x):
        at = which * features + wide * group
        grad_ref[:, at : at + wide] = x.astype(jnp.bfloat16)

    for group in range(HEADS // GROUP):
        grad_mixed = fanned(part(mixed_ref, 0, group))
        slopes_ref[group] = across(part(proj_ref, 2, group), grad_mixed)
        put(2, group, matmul(low_ref[group], grad_mixed))

    for group in range(HEADS // GROUP):
        probs, grad_probs = scores_ref[group], slopes_ref[group]
        along = jnp.sum(grad_probs * probs, axis=0, keepdims=True)
        low_ref[group] = (probs * (grad_probs - along)).astype(jnp.bfloat16)

    for group in range(HEADS // GROUP):
        put(0, group, gathered(low_ref[group], part(proj_ref, 1, group)))
        put(1, group, matmul(low_ref[group], wide_query[group]))

    grad_tokens = matmul(grad_ref[...], qkv_turned[...]).astype(jnp.bfloat16).astype(jnp.float32)
    cots[...] = cots[...] + grad_tokens

    for k, ref in enumerate(results):
        for f, source in enumerate((tokens, cots)):
            for r in range(rows):
                for c in range(cols):
                    at = k * quarter + (r * cols + c) * levels
                    ref[f, r, c] = source[at : at + levels, :].astype(jnp.bfloat16)


def body(latent, cotangent, norm_gain, qkv_weight, out_weight):
    levels, rows, cols, features = latent.shape
    assert (rows, cols) == (WLAT, WLON) and (2 * SLAT, 2 * SLON) == (WLAT, WLON)
    window = levels * rows * cols
    quarter = (2, SLAT, SLON, levels, features)
    packed = (HEADS // GROUP, window, GROUP * window)
    in_vmem = pl.BlockSpec(memory_space=pltpu.VMEM)
    in_hbm = pl.BlockSpec(memory_space=pltpu.HBM)
    piece = pltpu.VMEM(quarter, jnp.bfloat16)
    few = pltpu.CompilerParams(vmem_limit_bytes=MIB)
    latent, cotangent = latent.transpose(1, 2, 0, 3), cotangent.transpose(1, 2, 0, 3)

    to_both, to_lat, to_lon = pl.pallas_call(
        cut_kernel,
        in_specs=[in_hbm] * 2,
        out_specs=[in_vmem] * 3,
        out_shape=[piece] * 3,
        scratch_shapes=[pltpu.SemaphoreType.DMA((3, 2))],
        compiler_params=few,
        name="cut",
    )(stay(latent), stay(cotangent))

    from_both = neighbour(to_both, LAT_STEP, LON_STEP)
    from_lat = neighbour(to_lat, LAT_STEP, 0)
    from_lon = neighbour(to_lon, 0, LON_STEP)

    own, *parameters = pl.pallas_call(
        fetch_kernel,
        in_specs=[in_hbm] * 5,
        out_specs=[in_vmem] * 6,
        out_shape=[
            piece,
            pltpu.VMEM((1, features), jnp.float32),
            pltpu.VMEM(qkv_weight.shape, jnp.bfloat16),
            pltpu.VMEM(out_weight.shape, jnp.bfloat16),
            pltpu.VMEM(qkv_weight.shape[::-1], jnp.bfloat16),
            pltpu.VMEM(out_weight.shape[::-1], jnp.bfloat16),
        ],
        scratch_shapes=[pltpu.SemaphoreType.DMA((2 * features // STRIP + 3,))],
        compiler_params=few,
        cost_estimate=pl.CostEstimate(flops=0, bytes_accessed=4 * MIB, transcendentals=0),
        name="fetch",
    )(*map(stay, (latent, cotangent, norm_gain.reshape(1, features), qkv_weight, out_weight)))

    to_both, to_lat, to_lon, own = pl.pallas_call(
        window_kernel,
        in_specs=[in_vmem] * 9,
        out_specs=[in_vmem] * 4,
        out_shape=[piece] * 4,
        scratch_shapes=[
            pltpu.VMEM((window, features), jnp.float32),
            pltpu.VMEM((window, features), jnp.float32),
            pltpu.VMEM(packed, jnp.float32),
            pltpu.VMEM(packed, jnp.bfloat16),
            pltpu.VMEM(packed, jnp.float32),
            pltpu.VMEM((HEADS // GROUP, GROUP * window, features * GROUP // HEADS), jnp.bfloat16),
            pltpu.VMEM((window, 3 * features), jnp.bfloat16),
            pltpu.VMEM((window, features), jnp.bfloat16),
            pltpu.VMEM((window, 3 * features), jnp.bfloat16),
        ],
        compiler_params=pltpu.CompilerParams(vmem_limit_bytes=12 * MIB),
        name="window",
    )(from_lat, from_both, from_lon, own, *parameters)

    from_both = neighbour(to_both, -LAT_STEP, -LON_STEP)
    from_lat = neighbour(to_lat, -LAT_STEP, 0)
    from_lon = neighbour(to_lon, 0, -LON_STEP)

    def join(which, quarters, outs=()):
        return pl.pallas_call(
            functools.partial(join_kernel, which),
            in_specs=[in_vmem] * len(which) + [in_hbm] * len(outs),
            out_specs=[in_hbm] * 2,
            out_shape=[pltpu.HBM((rows, cols, levels, features), jnp.bfloat16)] * 2,
            scratch_shapes=[pltpu.SemaphoreType.DMA((len(which), 2))],
            input_output_aliases={len(which) + f: f for f in range(len(outs))},
            compiler_params=few,
            name="join",
        )(*quarters, *outs)

    outs = join((3,), (own,))
    updated, latent_grad = join((0, 2, 1), (from_both, from_lon, from_lat), tuple(outs))
    return (updated.transpose(2, 0, 1, 3), latent_grad.transpose(2, 0, 1, 3))


def solution(mesh):
    placed = (P(None, "lat", "lon", None), P(None, "lat", "lon", None), P(), P(), P())
    return jax.shard_map(
        body,
        mesh=mesh,
        in_specs=placed,
        out_specs=(P(None, "lat", "lon", None), P(None, "lat", "lon", None)),
        check_vma=False,
    )
```

```python
import functools
import math

import jax
import jax.numpy as jnp
from jax import lax
from jax.experimental import pallas as pl
from jax.experimental.pallas import tpu as pltpu
from jax.sharding import PartitionSpec as P

HEADS = 8
WLAT = 12
WLON = 6
SLAT = 6
SLON = 3
GROUP = 4
STRIP = 512

MIB = 1 << 20
NORM_EPS = 1e-05
MASK_FILL = -1000000000.0

LAT_STEP = 1
LON_STEP = -1


def neighbour(piece, lat_by, lon_by):
    lats, lons = lax.axis_size("lat"), lax.axis_size("lon")
    pairs = [
        (i * lons + j, (i + lat_by) % lats * lons + (j + lon_by) % lons)
        for i in range(lats)
        for j in range(lons)
    ]
    return lax.ppermute(piece, ("lat", "lon"), pairs)


def corners(rows, cols):
    early_rows, late_rows = pl.ds(0, SLAT), pl.ds(SLAT, rows - SLAT)
    early_cols, late_cols = pl.ds(0, SLON), pl.ds(SLON, cols - SLON)
    go_rows, stay_rows = (early_rows, late_rows) if LAT_STEP < 0 else (late_rows, early_rows)
    go_cols, stay_cols = (early_cols, late_cols) if LON_STEP < 0 else (late_cols, early_cols)
    return (
        (go_rows, go_cols), (go_rows, stay_cols), (stay_rows, go_cols), (stay_rows, stay_cols)
    )


def stay(x):
    return pltpu.with_memory_space_constraint(x, pltpu.HBM)


def cut_kernel(latent, cotangent, *rest):
    pieces, sems = rest[:3], rest[3]
    copies = []
    for k, (rows, cols) in enumerate(corners(*latent.shape[:2])[:3]):
        for f, field in enumerate((latent, cotangent)):
            copies.append(
                pltpu.make_async_copy(field.at[rows, cols], pieces[k].at[f], sems.at[k, f])
            )
    for copy in copies:
        copy.start()
    for copy in copies:
        copy.wait()


def fetch_kernel(
    latent, cotangent, gain, qkv, out, own, gain_to, qkv_to, out_to, qkv_turned, out_turned, sems
):
    rows, cols = corners(*latent.shape[:2])[3]
    width = out.shape[1]
    scale = 1.0 / math.sqrt(width // HEADS)
    pieces = []
    for source, into, turned in ((out, out_to, out_turned), (qkv, qkv_to, qkv_turned)):
        for at in range(0, source.shape[0], STRIP):
            pieces.append((source, into, turned, pl.ds(at, STRIP)))
    strips = [
        pltpu.make_async_copy(source.at[at], into.at[at], sems.at[k])
        for k, (source, into, _, at) in enumerate(pieces)
    ]
    others = [
        pltpu.make_async_copy(gain, gain_to, sems.at[len(strips)]),
        pltpu.make_async_copy(latent.at[rows, cols], own.at[0], sems.at[len(strips) + 1]),
        pltpu.make_async_copy(cotangent.at[rows, cols], own.at[1], sems.at[len(strips) + 2]),
    ]
    for copy in strips + others:
        copy.start()
    for copy, (_, into, turned, at) in zip(strips, pieces):
        copy.wait()
        if into is qkv_to:
            into[at, :width] = into[at, :width] * jnp.asarray(scale, jnp.bfloat16)
        turned[:, at] = into[at].T
    for copy in others:
        copy.wait()


def join_kernel(which, *refs):
    quarters, outs, sems = refs[: len(which)], refs[-3:-1], refs[-1]
    places = corners(*outs[0].shape[:2])
    copies = []
    for k, place in enumerate(which):
        for f, field in enumerate(outs):
            rows, cols = places[place]
            copies.append(
                pltpu.make_async_copy(quarters[k].at[f], field.at[rows, cols], sems.at[k, f])
            )
    for copy in copies:
        copy.start()
    for copy in copies:
        copy.wait()


def across(a, b):
    return lax.dot_general(a, b, (((1,), (1,)), ((), ())), preferred_element_type=jnp.float32)


def down(a, b):
    return lax.dot_general(a, b, (((0,), (0,)), ((), ())), preferred_element_type=jnp.float32)


def matmul(a, b):
    return jnp.dot(a, b, preferred_element_type=jnp.float32)


def window_kernel(
    ahead_lat, ahead_both, ahead_lon, own, gain_ref, qkv_ref, out_ref, qkv_turned, out_turned,
    both_out, lat_out, lon_out, own_out,
    tokens, cots, scores_ref, low_ref, slopes_ref, wide_query, proj_ref, mixed_ref, grad_ref,
):
    quarters = (ahead_both, ahead_lat, ahead_lon, own)
    results = (both_out, lat_out, lon_out, own_out)
    _, rows, cols, levels, features = own.shape
    quarter = rows * cols * levels
    window = 4 * quarter
    head_dim = features // HEADS

    for k, ref in enumerate(quarters):
        for f, into in enumerate((tokens, cots)):
            for r in range(rows):
                for c in range(cols):
                    at = k * quarter + (r * cols + c) * levels
                    into[at : at + levels, :] = ref[f, r, c].astype(jnp.float32)

    proj_ref[...] = matmul(tokens[...].astype(jnp.bfloat16), qkv_ref[...]).astype(jnp.bfloat16)

    last = lax.axis_index("lat") == (lax.axis_size("lat") - 1 if LAT_STEP < 0 else 0)
    wide = GROUP * head_dim
    packed = GROUP * window
    key_row = lax.broadcasted_iota(jnp.int32, (window, packed), 0)
    query_row = lax.rem(lax.broadcasted_iota(jnp.int32, (window, packed), 1), window)
    fill = jnp.where(last, MASK_FILL, 0.0).astype(jnp.float32)
    bias = jnp.where((key_row < 2 * quarter) != (query_row < 2 * quarter), fill, 0.0)
    lane = lax.broadcasted_iota(jnp.int32, (1, wide), 1)
    only = [(lane // head_dim == e).astype(jnp.float32).astype(jnp.bfloat16) for e in range(GROUP)]
    first = lax.broadcasted_iota(jnp.int32, (window, 2 * head_dim), 1) < head_dim

    def part(ref, which, group):
        at = which * features + wide * group
        return ref[:, at : at + wide]

    def fanned(x):
        return jnp.concatenate([x * only[e] for e in range(GROUP)], axis=0)

    def gathered(packed_rows, x):
        rows_first, parts = packed_rows.T, []
        for pair in range(GROUP // 2):
            lanes = slice(2 * head_dim * pair, 2 * head_dim * (pair + 1))
            both = matmul(rows_first[2 * window * pair : 2 * window * (pair + 1)], x[:, lanes])
            parts.append(jnp.where(first, both[:window], both[window:]))
        return jnp.concatenate(parts, axis=1)

    for group in range(HEADS // GROUP):
        wide_query[group] = fanned(part(proj_ref, 0, group))
        scores_ref[group] = across(part(proj_ref, 1, group), wide_query[group])

    for group in range(HEADS // GROUP):
        scores = scores_ref[group] + bias
        grown = jnp.exp(scores - jnp.max(scores, axis=0, keepdims=True))
        probs = grown * (1.0 / jnp.sum(grown, axis=0, keepdims=True))
        scores_ref[group] = probs
        low_ref[group] = probs.astype(jnp.bfloat16)

    for group in range(HEADS // GROUP):
        at = wide * group
        mixed = gathered(low_ref[group], part(proj_ref, 2, group))
        mixed_ref[:, at : at + wide] = mixed.astype(jnp.bfloat16)

    branch = matmul(mixed_ref[...], out_ref[...]).astype(jnp.bfloat16).astype(jnp.float32)
    gain = gain_ref[...]
    upstream = gain * cots[...]
    centre_up = jnp.mean(upstream, axis=-1, keepdims=True)
    centred = branch - jnp.mean(branch, axis=-1, keepdims=True)
    spread = jnp.mean(centred * centred, axis=-1, keepdims=True)
    along = jnp.mean(upstream * centred, axis=-1, keepdims=True)
    inverse = lax.rsqrt(spread + NORM_EPS)
    normed = centred * inverse
    tokens[...] = tokens[...] + gain * normed
    grad_branch = (inverse * (upstream - centre_up - normed * (along * inverse))).astype(jnp.bfloat16)
    mixed_ref[...] = matmul(grad_branch, out_turned[...]).astype(jnp.bfloat16)

    def put(which, group, x):
        at = which * features + wide * group
        grad_ref[:, at : at + wide] = x.astype(jnp.bfloat16)

    for group in range(HEADS // GROUP):
        grad_mixed = fanned(part(mixed_ref, 0, group))
        slopes_ref[group] = across(part(proj_ref, 2, group), grad_mixed)
        put(2, group, matmul(low_ref[group], grad_mixed))

    for group in range(HEADS // GROUP):
        probs, grad_probs = scores_ref[group], slopes_ref[group]
        along = jnp.sum(grad_probs * probs, axis=0, keepdims=True)
        low_ref[group] = (probs * (grad_probs - along)).astype(jnp.bfloat16)

    for group in range(HEADS // GROUP):
        put(0, group, gathered(low_ref[group], part(proj_ref, 1, group)))
        put(1, group, matmul(low_ref[group], wide_query[group]))

    grad_tokens = matmul(grad_ref[...], qkv_turned[...]).astype(jnp.bfloat16).astype(jnp.float32)
    cots[...] = cots[...] + grad_tokens

    for k, ref in enumerate(results):
        for f, source in enumerate((tokens, cots)):
            for r in range(rows):
                for c in range(cols):
                    at = k * quarter + (r * cols + c) * levels
                    ref[f, r, c] = source[at : at + levels, :].astype(jnp.bfloat16)


def body(latent, cotangent, norm_gain, qkv_weight, out_weight):
    levels, rows, cols, features = latent.shape
    assert (rows, cols) == (WLAT, WLON) and (2 * SLAT, 2 * SLON) == (WLAT, WLON)
    window = levels * rows * cols
    quarter = (2, SLAT, SLON, levels, features)
    packed = (HEADS // GROUP, window, GROUP * window)
    in_vmem = pl.BlockSpec(memory_space=pltpu.VMEM)
    in_hbm = pl.BlockSpec(memory_space=pltpu.HBM)
    piece = pltpu.VMEM(quarter, jnp.bfloat16)
    few = pltpu.CompilerParams(vmem_limit_bytes=MIB)
    latent, cotangent = latent.transpose(1, 2, 0, 3), cotangent.transpose(1, 2, 0, 3)

    to_both, to_lat, to_lon = pl.pallas_call(
        cut_kernel,
        in_specs=[in_hbm] * 2,
        out_specs=[in_vmem] * 3,
        out_shape=[piece] * 3,
        scratch_shapes=[pltpu.SemaphoreType.DMA((3, 2))],
        compiler_params=few,
        name="cut",
    )(stay(latent), stay(cotangent))

    from_both = neighbour(to_both, LAT_STEP, LON_STEP)
    from_lat = neighbour(to_lat, LAT_STEP, 0)
    from_lon = neighbour(to_lon, 0, LON_STEP)

    own, *parameters = pl.pallas_call(
        fetch_kernel,
        in_specs=[in_hbm] * 5,
        out_specs=[in_vmem] * 6,
        out_shape=[
            piece,
            pltpu.VMEM((1, features), jnp.float32),
            pltpu.VMEM(qkv_weight.shape, jnp.bfloat16),
            pltpu.VMEM(out_weight.shape, jnp.bfloat16),
            pltpu.VMEM(qkv_weight.shape[::-1], jnp.bfloat16),
            pltpu.VMEM(out_weight.shape[::-1], jnp.bfloat16),
        ],
        scratch_shapes=[pltpu.SemaphoreType.DMA((2 * features // STRIP + 3,))],
        compiler_params=few,
        cost_estimate=pl.CostEstimate(flops=0, bytes_accessed=4 * MIB, transcendentals=0),
        name="fetch",
    )(*map(stay, (latent, cotangent, norm_gain.reshape(1, features), qkv_weight, out_weight)))

    to_both, to_lat, to_lon, own = pl.pallas_call(
        window_kernel,
        in_specs=[in_vmem] * 9,
        out_specs=[in_vmem] * 4,
        out_shape=[piece] * 4,
        scratch_shapes=[
            pltpu.VMEM((window, features), jnp.float32),
            pltpu.VMEM((window, features), jnp.float32),
            pltpu.VMEM(packed, jnp.float32),
            pltpu.VMEM(packed, jnp.bfloat16),
            pltpu.VMEM(packed, jnp.float32),
            pltpu.VMEM((HEADS // GROUP, GROUP * window, features * GROUP // HEADS), jnp.bfloat16),
            pltpu.VMEM((window, 3 * features), jnp.bfloat16),
            pltpu.VMEM((window, features), jnp.bfloat16),
            pltpu.VMEM((window, 3 * features), jnp.bfloat16),
        ],
        compiler_params=pltpu.CompilerParams(vmem_limit_bytes=12 * MIB),
        name="window",
    )(from_lat, from_both, from_lon, own, *parameters)

    from_both = neighbour(to_both, -LAT_STEP, -LON_STEP)
    from_lat = neighbour(to_lat, -LAT_STEP, 0)
    from_lon = neighbour(to_lon, 0, -LON_STEP)

    def join(which, quarters, outs=()):
        return pl.pallas_call(
            functools.partial(join_kernel, which),
            in_specs=[in_vmem] * len(which) + [in_hbm] * len(outs),
            out_specs=[in_hbm] * 2,
            out_shape=[pltpu.HBM((rows, cols, levels, features), jnp.bfloat16)] * 2,
            scratch_shapes=[pltpu.SemaphoreType.DMA((len(which), 2))],
            input_output_aliases={len(which) + f: f for f in range(len(outs))},
            compiler_params=few,
            name="join",
        )(*quarters, *outs)

    outs = join((3,), (own,))
    updated, latent_grad = join((0, 2, 1), (from_both, from_lon, from_lat), tuple(outs))
    return (updated.transpose(2, 0, 1, 3), latent_grad.transpose(2, 0, 1, 3))


def solution(mesh):
    placed = (P(None, "lat", "lon", None), P(None, "lat", "lon", None), P(), P(), P())
    return jax.shard_map(
        body,
        mesh=mesh,
        in_specs=placed,
        out_specs=(P(None, "lat", "lon", None), P(None, "lat", "lon", None)),
        check_vma=False,
    )
```
